512 devices in a mesh: member: 32 (over y_lo, z), fsdp: 16 (over x, y_hi, core).
Axes of the slice: x: 4, y: 4 (y_hi: 2, y_lo: 2; y = y_hi * 2 + y_lo), z: 16, core: 2. Of those that a mesh axis runs over, the one named last changes fastest.
Arguments:
- inputs: bfloat16 [32, 2048, 1792], P('member', 'fsdp'), may hold values from -6 to 6
- queries: bfloat16 [32, 2048, 2048], P('member', 'fsdp'), may hold values from -6 to 6
- keys: bfloat16 [32, 2048, 1024], P('member', 'fsdp'), may hold values from -6 to 6
- cotangent: bfloat16 [32, 2048, 2048], P('member', 'fsdp'), may hold values from -6 to 6
- winners: int32 [32], replicated, may hold values from 0 to 31, as said below
- weights: bfloat16 [32, 1792, 1024], P('member', 'fsdp'), may hold values from -0.125 to 0.125
- first_moment: float32 [32, 1792, 1024], P('member', 'fsdp'), may hold values from -4 to 4
- second_moment: float32 [32, 1792, 1024], P('member', 'fsdp'), may hold values from 0.001 to 1
Outputs:
- new_weights: bfloat16 [32, 1792, 1024], P('member', 'fsdp')
- new_first: float32 [32, 1792, 1024], P('member', 'fsdp')
- new_second: float32 [32, 1792, 1024], P('member', 'fsdp')
The draws below stay inside these ranges and needn't reach their ends.
Inputs may be any that keep to these rules, and one draw needn't show every extreme that they name: winners[i] == i for the members that keep their state; the other 8 members name a member that keeps its own, and one member may be named by several.
All inputs are finite; a program needn't handle non-finite values.
Results may differ from the reference program's by a relative error of at most 0.015.
Values may be sent and summed in bfloat16 or wider, within the bound.
A program may use at most 64 MiB of HBM per device.

```python
import math
import jax
import jax.numpy as jnp
from jax import lax

D = 1792
HEADS = 8
KV_HEADS = 4
HEAD_DIM = 256
TOK_DEV = 128
SEQS = 1
KVW = 1024
QW = 2048
MEMBERS = 32
TOKENS = 2048


def draw_winners(key, part):
    key = jax.random.fold_in(key, 7)
    order_key, pick_key = jax.random.split(key)
    quarter = max(MEMBERS // 4, 1)
    order = jax.random.permutation(order_key, MEMBERS)
    losers = order[:quarter]
    keepers = order[MEMBERS - quarter:]
    picks = jax.random.randint(pick_key, (quarter,), 0, quarter)
    sources = keepers[picks]
    winners = jnp.arange(MEMBERS, dtype=jnp.int32).at[losers].set(sources.astype(jnp.int32))
    return winners.astype(jnp.int32)


def with_spikes(drawn, rng, source, target, blocks, factor):
    owner, partner = [(jnp.arange(drawn.shape[dim]) // (drawn.shape[dim] // blocks)).reshape([-1 if axis == dim else 1 for axis in range(drawn.ndim)]) for dim in (source, target)]
    chosen = jax.random.permutation(rng, blocks)[partner]
    strong = (owner == chosen) | (owner == (partner + blocks // 2) % blocks)
    return jnp.where(strong, factor * drawn, drawn)


def block_levels(key, shape, cuts, low, largest):
    factor_of = 1.0
    for position, blocks in cuts:
        steps = jax.random.uniform(jax.random.fold_in(jax.random.fold_in(key, 6), position), (blocks,), jnp.float32, low / len(cuts), largest / len(cuts))
        factor_of = factor_of * jnp.repeat(jnp.exp(steps), shape[position] // blocks).reshape((-1,) + (1,) * (len(shape) - 1 - position))
    return factor_of


def scatter_about(rng, shape, scale, most, pieces=(), kind=jnp.bfloat16):
    values = jax.random.normal(rng, shape, jnp.float32) * scale
    if len(pieces) > 0:
        values = block_levels(rng, shape, pieces, -0.22, 0.18) * values
    return jnp.clip(values, min=-most, max=most).astype(kind)


def heavy_noise(own_key, shape, scale, bound, cuts, heavy, kind=jnp.bfloat16):
    drawn = scale * jax.random.normal(own_key, shape, jnp.float32)
    if cuts:
        drawn = drawn * block_levels(own_key, shape, cuts, -0.22, 0.18)
    return jnp.clip(with_spikes(drawn, jax.random.fold_in(own_key, 3), *heavy), -bound, bound).astype(kind)


def setup_inputs(seed: int = 0) -> dict:
    splits = jax.random.split(jax.random.key(seed), 9)
    inputs = heavy_noise(splits[0], (MEMBERS, TOKENS, D), 1.0, 6.0, ((0, 32), (1, 16)), (1, 2, 16, 2.0))
    queries = scatter_about(splits[1], (MEMBERS, TOKENS, QW), 1.0, 6.0, ((0, 32), (1, 16)))
    keys = scatter_about(splits[2], (MEMBERS, TOKENS, KVW), 1.0, 6.0, ((0, 32), (1, 16)))
    cotangent = scatter_about(splits[3], (MEMBERS, TOKENS, QW), 0.5, 6.0, ((0, 32), (1, 16)))
    winners = draw_winners(jax.random.fold_in(splits[8], 71), 0)
    weights = scatter_about(splits[5], (MEMBERS, D, KVW), D ** -0.5, 0.125, ((0, 32), (1, 16)))
    first_moment = scatter_about(splits[6], (MEMBERS, D, KVW), 0.3, 4.0, ((0, 32), (1, 16)), jnp.float32)
    second_moment = jnp.clip(jnp.exp(math.log(1.0) - 6.9077552 * jax.random.uniform(splits[7], (MEMBERS, D, KVW), jnp.float32) ** block_levels(splits[7], (MEMBERS, D, KVW), ((0, 32), (1, 16)), -0.2, 0.2)), 0.001, 1.0)
    return dict(inputs=inputs, queries=queries, keys=keys, cotangent=cotangent, winners=winners, weights=weights, first_moment=first_moment, second_moment=second_moment)


beta_one = 0.9
beta_two = 0.999
learning_rate = 0.001
decay_rate = 0.1
adam_eps = 1e-08
adam_step = 200
soft_cap = 50.0

def block_gradient(inputs, queries, keys, cotangent, block_index):
    seq_len = TOKENS // SEQS
    groups = HEADS // KV_HEADS
    score_scale = HEAD_DIM ** (-0.5)
    first_row = block_index * TOK_DEV
    seq_begin = first_row // seq_len * seq_len
    query_heads = lax.dynamic_slice_in_dim(queries, first_row, TOK_DEV, 0).reshape(TOK_DEV, KV_HEADS, groups, HEAD_DIM)
    grad_heads = lax.dynamic_slice_in_dim(cotangent, first_row, TOK_DEV, 0).reshape(TOK_DEV, KV_HEADS, groups, HEAD_DIM)
    key_heads = lax.dynamic_slice_in_dim(keys, seq_begin, seq_len, 0).reshape(seq_len, KV_HEADS, HEAD_DIM)
    value_rows = lax.dynamic_slice_in_dim(inputs, seq_begin, seq_len, 0)
    scores = jnp.einsum('rkgd,nkd->kgrn', query_heads.astype(jnp.float32), key_heads.astype(jnp.float32)) * score_scale
    capped = soft_cap * jnp.tanh(scores / soft_cap)
    query_pos = first_row + jnp.arange(TOK_DEV, dtype=jnp.int32)
    key_pos = seq_begin + jnp.arange(seq_len, dtype=jnp.int32)
    allowed = key_pos[None, :] <= query_pos[:, None]
    weights_exp = jnp.where(allowed, jnp.exp(capped), jnp.zeros_like(capped))
    expo_low = weights_exp.astype(jnp.bfloat16)
    numerator = jnp.einsum('kgrn,nc->kgrc', expo_low.astype(jnp.float32), value_rows.astype(jnp.float32))
    denominator = lax.optimization_barrier(jnp.sum(weights_exp, axis=-1))
    mixed = (numerator / denominator[..., None]).astype(jnp.bfloat16)
    partial_value = jnp.einsum('kgrc,rkgd->ckd', mixed.astype(jnp.float32), grad_heads.astype(jnp.float32))
    rounded = lax.optimization_barrier(partial_value.reshape(D, KV_HEADS * HEAD_DIM).astype(jnp.bfloat16))
    return rounded.astype(jnp.float32)

def member_gradient(inputs, queries, keys, cotangent):

    def add_block(total, block_index):
        return (total + block_gradient(inputs, queries, keys, cotangent, block_index), block_index)
    start_total = jnp.zeros((D, KV_HEADS * HEAD_DIM), jnp.float32)
    total, ignored = lax.scan(add_block, start_total, jnp.arange(TOKENS // TOK_DEV, dtype=jnp.int32))
    return total

def reference(inputs, queries, keys, cotangent, winners, weights, first_moment, second_moment):
    gradient = lax.map(lambda member_data: member_gradient(member_data[0], member_data[1], member_data[2], member_data[3]), (inputs, queries, keys, cotangent))
    source_weights = weights[winners].astype(jnp.float32)
    source_first = first_moment[winners]
    source_second = second_moment[winners]
    new_first = beta_one * source_first + (1.0 - beta_one) * gradient
    new_second = beta_two * source_second + (1.0 - beta_two) * gradient * gradient
    first_hat = new_first / (1.0 - beta_one ** adam_step)
    second_hat = new_second / (1.0 - beta_two ** adam_step)
    update = first_hat / (jnp.sqrt(second_hat) + adam_eps) + decay_rate * source_weights
    new_weights = (source_weights - learning_rate * update).astype(jnp.bfloat16)
    return (new_weights, new_first, new_second)
```

```python
import jax
import jax.numpy as jnp
from jax import lax
from jax.experimental import pallas as pl
from jax.experimental.pallas import tpu as pltpu
from jax.sharding import PartitionSpec as P

MEMBERS = 32
KV_HEADS = 4
QUARTERS = 4
HEAD_DIM = 256
GROUP_HEADS = 2
TOK = 128
FEAT = 1792
ROWS = 112
KVW = 1024
PART = QUARTERS * TOK
PIECE = 48
BANDS = 7

beta_one = 0.9
beta_two = 0.999
learning_rate = 0.001
decay_rate = 0.1
adam_eps = 1e-08
adam_step = 200
soft_cap = 50.0

MESH = pl.DeviceIdType.MESH


def kernel(
    winners, x_in, q_in, k_in, c_in, w_in, m_in, v_in,
    new_w, new_m, new_v,
    k_all, q_g, c_g, x_g, x_t, expo, denom, cots,
    dv_acc, dv_out, dv_in, gr_acc, gr_out, gr_in, sum_out, grad,
    state, dealt, picked, source,
    loc_sem, grp_send, grp_recv, key_send, key_recv, dv_send, dv_recv,
    gr_send, gr_recv, own_send, own_recv, deal_send, deal_recv, pick_send, pick_recv,
):
    me = lax.axis_index("member")
    mine = lax.axis_index("fsdp")
    j = mine // KV_HEADS
    g = mine % KV_HEADS

    barrier = pltpu.get_barrier_semaphore()
    for s in range(1, 4):
        pl.semaphore_signal(
            barrier, inc=1, device_id={"fsdp": j * 4 + (g + s) % 4}, device_id_type=MESH
        )
        pl.semaphore_signal(
            barrier, inc=1, device_id={"fsdp": (j + s) % 4 * 4 + g}, device_id_type=MESH
        )

    @pl.loop(1, MEMBERS)
    def _(s):
        pl.semaphore_signal(
            barrier, inc=1, device_id={"member": (me + s) % MEMBERS}, device_id_type=MESH
        )

    def own_slot(kind, owner):
        rows = pl.ds(owner * TOK, TOK)
        return (k_all.at[j, rows], q_g.at[rows], c_g.at[rows], x_g.at[rows])[kind]

    def own_slice(kind, head):
        if kind == 0:
            return k_in.at[:, pl.ds(head * HEAD_DIM, HEAD_DIM)]
        if kind == 3:
            return x_in
        wide = GROUP_HEADS * HEAD_DIM
        return (q_in, c_in)[kind - 1].at[:, pl.ds(head * wide, wide)]

    def group_copy(kind, s):
        peer = (g + s) % 4
        return pltpu.make_async_remote_copy(
            src_ref=own_slice(kind, peer),
            dst_ref=own_slot(kind, g),
            send_sem=grp_send.at[kind, s],
            recv_sem=grp_recv.at[kind, s],
            device_id={"fsdp": j * 4 + peer},
            device_id_type=MESH,
        )

    def group_wait(kind):
        for s in range(1, 4):
            slot = own_slot(kind, (g + 4 - s) % 4)
            pltpu.make_async_remote_copy(
                src_ref=slot,
                dst_ref=slot,
                send_sem=grp_send.at[kind, s],
                recv_sem=grp_recv.at[kind, s],
                device_id={"fsdp": j * 4 + (g + s) % 4},
                device_id_type=MESH,
            ).wait_recv()
        local_copy(kind).wait()

    def local_copy(kind):
        return pltpu.make_async_copy(own_slice(kind, g), own_slot(kind, g), loc_sem.at[kind])

    for kind in range(4):
        local_copy(kind).start()

    for band in range(4):
        cols = slice(band * 256, (band + 1) * 256)
        state[band, 0:ROWS] = w_in[:, cols]
        state[band, ROWS : 2 * ROWS] = m_in[:, cols].astype(jnp.bfloat16)
        state[band, 2 * ROWS : 3 * ROWS] = v_in[:, cols].astype(jnp.bfloat16)

    pl.semaphore_wait(barrier, 6 + MEMBERS - 1)

    for kind in range(3):
        for s in range(1, 4):
            group_copy(kind, s).start()

    sorts = me % 8 != BANDS

    def place(ref, member):
        return ref.at[member // 8, pl.ds(member % 8 * PIECE, PIECE)]

    def deal_copy(s):
        peer = (me + s) % MEMBERS
        return pltpu.make_async_remote_copy(
            src_ref=place(state, peer),
            dst_ref=dealt.at[me],
            send_sem=deal_send.at[s],
            recv_sem=deal_recv.at[s],
            device_id={"member": peer},
            device_id_type=MESH,
        )

    @pl.loop(1, MEMBERS)
    def _(s):
        @pl.when((me + s) % 8 != BANDS)
        def _():
            deal_copy(s).start()

    for s in range(1, 4):
        group_copy(3, s).start()

    @pl.when(sorts)
    def _():
        dealt[me] = state[me // 8, pl.ds(me % 8 * PIECE, PIECE)]

    def key_copy(s):
        return pltpu.make_async_remote_copy(
            src_ref=k_all.at[j],
            dst_ref=k_all.at[j],
            send_sem=key_send.at[s],
            recv_sem=key_recv.at[s],
            device_id={"fsdp": (j + s) % 4 * 4 + g},
            device_id_type=MESH,
        )

    def key_wait(s):
        slot = k_all.at[(j + 4 - s) % 4]
        pltpu.make_async_remote_copy(
            src_ref=slot,
            dst_ref=slot,
            send_sem=key_send.at[s],
            recv_sem=key_recv.at[s],
            device_id={"fsdp": (j + s) % 4 * 4 + g},
            device_id_type=MESH,
        ).wait_recv()

    group_wait(0)
    for s in range(1, 4):

        @pl.when(j + s < 4)
        def _(s=s):
            key_copy(s).start()

    group_wait(1)
    denom[...] = jnp.zeros_like(denom)

    def scores(chunk, diagonal):
        @pl.loop(0, 4)
        def _(block):
            first = pl.multiple_of(block * TOK, TOK)
            key_block = k_all[chunk, pl.ds(first, TOK), :]
            for h in range(GROUP_HEADS):
                raw = lax.dot_general(
                    key_block,
                    q_g[:, h * HEAD_DIM : (h + 1) * HEAD_DIM],
                    (((1,), (1,)), ((), ())),
                    preferred_element_type=jnp.float32,
                )
                e = jnp.exp(soft_cap * jnp.tanh(raw * (HEAD_DIM**-0.5 / soft_cap)))
                if diagonal:
                    u = first + lax.broadcasted_iota(jnp.int32, (TOK, PART), 0)
                    t = lax.broadcasted_iota(jnp.int32, (TOK, PART), 1)
                    e = jnp.where(u <= t, e, 0.0)
                cols = slice(h * PART, (h + 1) * PART)
                expo[chunk, pl.ds(first, TOK), cols] = e.astype(jnp.bfloat16)
                denom[:, cols] += jnp.sum(e, axis=0, keepdims=True)

    scores(j, True)
    for s in range(1, 4):

        @pl.when(j >= s)
        def _(s=s):
            key_wait(s)
            scores(j - s, False)

    group_wait(2)
    for h in range(GROUP_HEADS):
        cols = slice(h * PART, (h + 1) * PART)
        inverse = jnp.transpose(jnp.broadcast_to(1.0 / denom[:, cols], (128, PART)))
        heads = c_g[:, h * HEAD_DIM : (h + 1) * HEAD_DIM].astype(jnp.float32)
        for half in range(2):
            lanes = slice(half * 128, (half + 1) * 128)
            cots[cols, lanes] = (heads[:, lanes] * inverse).astype(jnp.bfloat16)

    def dv_copy(s):
        return pltpu.make_async_remote_copy(
            src_ref=dv_out.at[s],
            dst_ref=dv_in.at[s],
            send_sem=dv_send.at[s],
            recv_sem=dv_recv.at[s],
            device_id={"fsdp": (j + 4 - s) % 4 * 4 + g},
            device_id_type=MESH,
        )

    for s in range(1, 4):

        @pl.when(j >= s)
        def _(s=s):
            dv_out[s] = jnp.dot(
                expo[j - s], cots[...], preferred_element_type=jnp.float32
            ).astype(jnp.bfloat16)
            dv_copy(s).start()

    dv_acc[...] = jnp.dot(expo[j], cots[...], preferred_element_type=jnp.float32)

    group_wait(3)

    @pl.loop(0, BANDS)
    def _(i):
        first = pl.multiple_of(i * 256, 256)
        x_t[pl.ds(first, 256), :] = jnp.transpose(x_g[:, pl.ds(first, 256)])

    def pick_copy(s):
        peer = (me + s) % MEMBERS
        return pltpu.make_async_remote_copy(
            src_ref=picked.at[s],
            dst_ref=place(source, me),
            send_sem=pick_send.at[s],
            recv_sem=pick_recv.at[s],
            device_id={"member": peer},
            device_id_type=MESH,
        )

    @pl.when(sorts)
    def _():
        @pl.loop(1, MEMBERS)
        def _(s):
            pltpu.make_async_remote_copy(
                src_ref=picked.at[s],
                dst_ref=dealt.at[(me + MEMBERS - s) % MEMBERS],
                send_sem=deal_send.at[s],
                recv_sem=deal_recv.at[s],
                device_id={"member": (me + s) % MEMBERS},
                device_id_type=MESH,
            ).wait_recv()

        @pl.loop(1, MEMBERS)
        def _(s):
            picked[s] = dealt[winners[(me + s) % MEMBERS]]
            pick_copy(s).start()

        source[me // 8, pl.ds(me % 8 * PIECE, PIECE)] = dealt[winners[me]]

    for s in range(1, 4):

        @pl.when(j + s < 4)
        def _(s=s):
            dv_copy(s).wait_recv()
            dv_acc[...] += dv_in[s].astype(jnp.float32)

    def gr_copy(s):
        return pltpu.make_async_remote_copy(
            src_ref=gr_out.at[s],
            dst_ref=gr_in.at[s],
            send_sem=gr_send.at[s],
            recv_sem=gr_recv.at[s],
            device_id={"fsdp": (j + s) % 4 * 4 + g},
            device_id_type=MESH,
        )

    dv_low = dv_acc[...].astype(jnp.bfloat16)

    def rows_of(quarter):
        first = pl.multiple_of(quarter * 4 * ROWS, 16)
        return jnp.dot(
            x_t[pl.ds(first, 4 * ROWS), :], dv_low, preferred_element_type=jnp.float32
        )

    for s in range(1, 4):
        gr_out[s] = rows_of((j + s) % 4).astype(jnp.bfloat16)
        gr_copy(s).start()
    gr_acc[...] = rows_of(j)
    for s in range(1, 4):
        gr_copy(s).wait_recv()
        gr_acc[...] += gr_in[s].astype(jnp.float32)
    sum_out[...] = gr_acc[...].astype(jnp.bfloat16)

    def own_copy(s):
        peer = (g + s) % 4
        return pltpu.make_async_remote_copy(
            src_ref=sum_out.at[pl.ds(peer * ROWS, ROWS)],
            dst_ref=grad.at[g],
            send_sem=own_send.at[s],
            recv_sem=own_recv.at[s],
            device_id={"fsdp": j * 4 + peer},
            device_id_type=MESH,
        )

    for s in range(1, 4):
        own_copy(s).start()
    grad[g] = sum_out[pl.ds(pl.multiple_of(g * ROWS, 16), ROWS), :]
    for s in range(1, 4):
        slot = grad.at[(g + 4 - s) % 4]
        pltpu.make_async_remote_copy(
            src_ref=slot,
            dst_ref=slot,
            send_sem=own_send.at[s],
            recv_sem=own_recv.at[s],
            device_id={"fsdp": j * 4 + (g + s) % 4},
            device_id_type=MESH,
        ).wait_recv()

    @pl.loop(1, MEMBERS)
    def _(s):
        peer = (me + MEMBERS - s) % MEMBERS

        @pl.when(peer % 8 != BANDS)
        def _():
            slot = place(source, peer)
            pltpu.make_async_remote_copy(
                src_ref=slot,
                dst_ref=slot,
                send_sem=pick_send.at[s],
                recv_sem=pick_recv.at[s],
                device_id={"member": (me + s) % MEMBERS},
                device_id_type=MESH,
            ).wait_recv()

    for band in range(4):
        cols = slice(band * 256, (band + 1) * 256)
        gradient = grad[band].astype(jnp.float32)
        old_w = source[band, 0:ROWS].astype(jnp.float32)
        old_m = source[band, ROWS : 2 * ROWS].astype(jnp.float32)
        old_v = source[band, 2 * ROWS : 3 * ROWS].astype(jnp.float32)
        first = beta_one * old_m + (1.0 - beta_one) * gradient
        second = beta_two * old_v + (1.0 - beta_two) * gradient * gradient
        first_hat = first * (1.0 / (1.0 - beta_one**adam_step))
        second_hat = second * (1.0 / (1.0 - beta_two**adam_step))
        update = first_hat / (jnp.sqrt(second_hat) + adam_eps) + decay_rate * old_w
        new_w[:, cols] = (old_w - learning_rate * update).astype(jnp.bfloat16)
        new_m[:, cols] = first
        new_v[:, cols] = second

    for kind in range(4):
        for s in range(1, 4):
            group_copy(kind, s).wait_send()
    for s in range(1, 4):

        @pl.when(j + s < 4)
        def _(s=s):
            key_copy(s).wait_send()

        @pl.when(j >= s)
        def _(s=s):
            dv_copy(s).wait_send()

        gr_copy(s).wait_send()
        own_copy(s).wait_send()

    @pl.loop(1, MEMBERS)
    def _(s):
        @pl.when((me + s) % 8 != BANDS)
        def _():
            deal_copy(s).wait_send()

        @pl.when(sorts)
        def _():
            pick_copy(s).wait_send()


def local(inputs, queries, keys, cotangent, winners, weights, first_moment, second_moment):
    f32, bf16 = jnp.float32, jnp.bfloat16
    vmem = pl.BlockSpec(memory_space=pltpu.VMEM)
    hbm = pl.BlockSpec(memory_space=pl.ANY)
    dma = pltpu.SemaphoreType.DMA
    outs = pl.pallas_call(
        kernel,
        out_shape=(
            jax.ShapeDtypeStruct((ROWS, KVW), bf16),
            jax.ShapeDtypeStruct((ROWS, KVW), f32),
            jax.ShapeDtypeStruct((ROWS, KVW), f32),
        ),
        in_specs=[pl.BlockSpec(memory_space=pltpu.SMEM), hbm, hbm, hbm, hbm, vmem, vmem, vmem],
        out_specs=(vmem, vmem, vmem),
        scratch_shapes=[
            pltpu.VMEM((QUARTERS, PART, HEAD_DIM), bf16),
            pltpu.VMEM((PART, GROUP_HEADS * HEAD_DIM), bf16),
            pltpu.VMEM((PART, GROUP_HEADS * HEAD_DIM), bf16),
            pltpu.VMEM((PART, FEAT), bf16),
            pltpu.VMEM((FEAT, PART), bf16),
            pltpu.VMEM((QUARTERS, PART, GROUP_HEADS * PART), bf16),
            pltpu.VMEM((1, GROUP_HEADS * PART), f32),
            pltpu.VMEM((GROUP_HEADS * PART, HEAD_DIM), bf16),
            pltpu.VMEM((PART, HEAD_DIM), f32),
            pltpu.VMEM((4, PART, HEAD_DIM), bf16),
            pltpu.VMEM((4, PART, HEAD_DIM), bf16),
            pltpu.VMEM((4 * ROWS, HEAD_DIM), f32),
            pltpu.VMEM((4, 4 * ROWS, HEAD_DIM), bf16),
            pltpu.VMEM((4, 4 * ROWS, HEAD_DIM), bf16),
            pltpu.VMEM((4 * ROWS, HEAD_DIM), bf16),
            pltpu.VMEM((4, ROWS, HEAD_DIM), bf16),
            pltpu.VMEM((4, 3 * ROWS, 256), bf16),
            pltpu.VMEM((MEMBERS, PIECE, 256), bf16),
            pltpu.VMEM((MEMBERS, PIECE, 256), bf16),
            pltpu.VMEM((4, 3 * ROWS, 256), bf16),
            dma((4,)),
            dma((4, 4)),
            dma((4, 4)),
            dma((4,)),
            dma((4,)),
            dma((4,)),
            dma((4,)),
            dma((4,)),
            dma((4,)),
            dma((4,)),
            dma((4,)),
            dma((MEMBERS,)),
            dma((MEMBERS,)),
            dma((MEMBERS,)),
            dma((MEMBERS,)),
        ],
        compiler_params=pltpu.CompilerParams(
            collective_id=0, has_side_effects=True, vmem_limit_bytes=48 * 1024 * 1024
        ),
        cost_estimate=pl.CostEstimate(
            flops=3_000_000_000, bytes_accessed=6_000_000, transcendentals=4_000_000
        ),
    )(
        winners, inputs[0], queries[0], keys[0], cotangent[0],
        weights[0], first_moment[0], second_moment[0],
    )
    return tuple(out[None] for out in outs)


def solution(mesh):
    rows = P("member", "fsdp", None)
    return jax.shard_map(
        local,
        mesh=mesh,
        in_specs=(rows, rows, rows, rows, P(), rows, rows, rows),
        out_specs=(rows, rows, rows),
        check_vma=False,
    )
```

```python
import jax
import jax.numpy as jnp
from jax import lax
from jax.experimental import pallas as pl
from jax.experimental.pallas import tpu as pltpu
from jax.sharding import PartitionSpec as P

MEMBERS = 32
KV_HEADS = 4
QUARTERS = 4
HEAD_DIM = 256
GROUP_HEADS = 2
TOK = 128
FEAT = 1792
ROWS = 112
KVW = 1024
PART = QUARTERS * TOK
PIECE = 80
BLOCKS = 7

beta_one = 0.9
beta_two = 0.999
learning_rate = 0.001
decay_rate = 0.1
adam_eps = 1e-08
adam_step = 200
soft_cap = 50.0

VMEM_LIMIT = 60 * 1024 * 1024

MESH = pl.DeviceIdType.MESH


def kernel(
    winners, x_in, q_in, k_in, c_in, w_in, m_in, v_in,
    grad_out, source_out,
    k_all, q_g, c_g, x_g, x_t, expo, denom, cots,
    dv_acc, dv_out, dv_in, gr_acc, gr_out, gr_in, sum_out, grad,
    w_own, m_own, v_own, state, dealt_0, dealt_1, dealt_2, picked_0, picked_1, picked_2, source,
    loc_sem, own_sem, out_sem, grp_send, grp_recv, key_send, key_recv, dv_send, dv_recv,
    gr_send, gr_recv, own_send, own_recv, fwd_send, fwd_recv, deal_send, deal_recv, pick_send, pick_recv,
):
    me = lax.axis_index("member")
    mine = lax.axis_index("fsdp")
    j = mine // KV_HEADS
    g = mine % KV_HEADS

    state_copies = [
        pltpu.make_async_copy(src, dst, own_sem.at[i])
        for i, (src, dst) in enumerate(((w_in, w_own), (m_in, m_own), (v_in, v_own)))
    ]
    for copy in state_copies:
        copy.start()

    barrier = pltpu.get_barrier_semaphore()
    for s in range(1, 4):
        pl.semaphore_signal(
            barrier, inc=1, device_id={"fsdp": j * 4 + (g + s) % 4}, device_id_type=MESH
        )
        pl.semaphore_signal(
            barrier, inc=1, device_id={"fsdp": (j + s) % 4 * 4 + g}, device_id_type=MESH
        )

    @pl.loop(1, MEMBERS)
    def _(s):
        pl.semaphore_signal(
            barrier, inc=1, device_id={"member": (me + s) % MEMBERS}, device_id_type=MESH
        )

    def own_slot(kind, owner):
        rows = pl.ds(owner * TOK, TOK)
        return (k_all.at[j, rows], q_g.at[rows], c_g.at[rows], x_g.at[rows])[kind]

    def own_slice(kind, head):
        if kind == 0:
            return k_in.at[:, pl.ds(head * HEAD_DIM, HEAD_DIM)]
        if kind == 3:
            return x_in
        wide = GROUP_HEADS * HEAD_DIM
        return (q_in, c_in)[kind - 1].at[:, pl.ds(head * wide, wide)]

    def group_copy(kind, s):
        peer = (g + s) % 4
        return pltpu.make_async_remote_copy(
            src_ref=own_slice(kind, peer),
            dst_ref=own_slot(kind, g),
            send_sem=grp_send.at[kind, s],
            recv_sem=grp_recv.at[kind, s],
            device_id={"fsdp": j * 4 + peer},
            device_id_type=MESH,
        )

    def group_wait(kind):
        for s in range(1, 4):
            slot = own_slot(kind, (g + 4 - s) % 4)
            pltpu.make_async_remote_copy(
                src_ref=slot,
                dst_ref=slot,
                send_sem=grp_send.at[kind, s],
                recv_sem=grp_recv.at[kind, s],
                device_id={"fsdp": j * 4 + (g + s) % 4},
                device_id_type=MESH,
            ).wait_recv()
        local_copy(kind).wait()

    def local_copy(kind):
        return pltpu.make_async_copy(own_slice(kind, g), own_slot(kind, g), loc_sem.at[kind])

    for kind in range(4):
        local_copy(kind).start()

    for copy in state_copies:
        copy.wait()
    for band in range(8):
        cols = slice(band * 128, (band + 1) * 128)
        state[band, 0:ROWS] = w_own[:, cols]
        state[band, ROWS : 2 * ROWS] = m_own[:, cols].astype(jnp.bfloat16)
        state[band, 2 * ROWS : 3 * ROWS] = v_own[:, cols].astype(jnp.bfloat16)

    pl.semaphore_wait(barrier, 6 + MEMBERS - 1)

    for kind in range(3):
        for s in range(1, 4):
            group_copy(kind, s).start()

    sibling = g + 1 - 2 * (g % 2)

    def x_copy(owner, peer, sem):
        slot = own_slot(3, owner)
        return pltpu.make_async_remote_copy(
            src_ref=x_in if sem < 2 else slot,
            dst_ref=slot,
            send_sem=fwd_send.at[sem],
            recv_sem=fwd_recv.at[sem],
            device_id={"fsdp": j * 4 + peer},
            device_id_type=MESH,
        )

    def x_wait(owner, sem):
        slot = own_slot(3, owner)
        pltpu.make_async_remote_copy(
            src_ref=slot,
            dst_ref=slot,
            send_sem=fwd_send.at[sem],
            recv_sem=fwd_recv.at[sem],
            device_id={"fsdp": j * 4 + sibling},
            device_id_type=MESH,
        ).wait_recv()

    core = mine % 2
    starts, sizes = (0, 48, 80), (48, 32, 16)
    dealt, picked = (dealt_0, dealt_1, dealt_2), (picked_0, picked_1, picked_2)

    def extra(member):
        return (member + 2 * core) % 4 == 1

    def sorts(member, part, action):
        if part < 2:
            action()
        else:
            pl.when(extra(member))(action)

    def place(ref, member, part):
        first = member % 4 * PIECE + starts[part] if part < 2 else 4 * PIECE
        return ref.at[member // 4, pl.ds(first, sizes[part])]

    def deal_copy(s, part):
        peer = (me + s) % MEMBERS
        return pltpu.make_async_remote_copy(
            src_ref=place(state, peer, part),
            dst_ref=dealt[part].at[me],
            send_sem=deal_send.at[part],
            recv_sem=deal_recv.at[part],
            device_id={"member": peer},
            device_id_type=MESH,
        )

    def all_of(part, count, send_sem, recv_sem):
        ref = dealt[part].at[pl.ds(0, count)]
        return pltpu.make_async_remote_copy(
            src_ref=ref,
            dst_ref=ref,
            send_sem=send_sem.at[part],
            recv_sem=recv_sem.at[part],
            device_id={"member": (me + 1) % MEMBERS},
            device_id_type=MESH,
        )

    def to_or_from_sorters(part, wait):
        if part < 2:
            wait(MEMBERS - 1)
        else:
            pl.when(extra(me))(lambda: wait(MEMBERS // 4 - 1))
            pl.when(jnp.logical_not(extra(me)))(lambda: wait(MEMBERS // 4))

    for part in range(3):

        @pl.loop(1, MEMBERS)
        def _(s):
            sorts((me + s) % MEMBERS, part, lambda: deal_copy(s, part).start())

    x_copy(g, sibling, 0).start()
    x_copy(g, (g + 2) % 4, 1).start()

    def keep(part):
        dealt[part][me] = place(state, me, part)[...]

    for part in range(3):
        sorts(me, part, lambda: keep(part))

    def pick_copy(s, part):
        peer = (me + s) % MEMBERS
        return pltpu.make_async_remote_copy(
            src_ref=picked[part].at[s],
            dst_ref=place(source, me, part),
            send_sem=pick_send.at[part],
            recv_sem=pick_recv.at[part],
            device_id={"member": peer},
            device_id_type=MESH,
        )

    def pick(part):
        def action():
            all_of(part, MEMBERS - 1, deal_send, deal_recv).wait_recv()

            @pl.loop(1, MEMBERS)
            def _(s):
                picked[part][s] = dealt[part][winners[(me + s) % MEMBERS]]
                pick_copy(s, part).start()

            place(source, me, part)[...] = dealt[part][winners[me]]

        sorts(me, part, action)

    def key_copy(s):
        return pltpu.make_async_remote_copy(
            src_ref=k_all.at[j],
            dst_ref=k_all.at[j],
            send_sem=key_send.at[s],
            recv_sem=key_recv.at[s],
            device_id={"fsdp": (j + s) % 4 * 4 + g},
            device_id_type=MESH,
        )

    def key_wait(s):
        slot = k_all.at[(j + 4 - s) % 4]
        pltpu.make_async_remote_copy(
            src_ref=slot,
            dst_ref=slot,
            send_sem=key_send.at[s],
            recv_sem=key_recv.at[s],
            device_id={"fsdp": (j + s) % 4 * 4 + g},
            device_id_type=MESH,
        ).wait_recv()

    group_wait(0)
    for s in range(1, 4):

        @pl.when(j + s < 4)
        def _(s=s):
            key_copy(s).start()

    group_wait(1)
    denom[...] = jnp.zeros_like(denom)

    def scores(chunk, diagonal):
        @pl.loop(0, 4)
        def _(block):
            first = pl.multiple_of(block * TOK, TOK)
            key_block = k_all[chunk, pl.ds(first, TOK), :]
            for h in range(GROUP_HEADS):
                raw = lax.dot_general(
                    key_block,
                    q_g[:, h * HEAD_DIM : (h + 1) * HEAD_DIM],
                    (((1,), (1,)), ((), ())),
                    preferred_element_type=jnp.float32,
                )
                e = jnp.exp(soft_cap * jnp.tanh(raw * (HEAD_DIM**-0.5 / soft_cap)))
                if diagonal:
                    u = first + lax.broadcasted_iota(jnp.int32, (TOK, PART), 0)
                    t = lax.broadcasted_iota(jnp.int32, (TOK, PART), 1)
                    e = jnp.where(u <= t, e, 0.0)
                cols = slice(h * PART, (h + 1) * PART)
                expo[chunk, pl.ds(first, TOK), cols] = e.astype(jnp.bfloat16)
                denom[:, cols] += jnp.sum(e, axis=0, keepdims=True)

    scores(j, True)
    for s in range(1, 4):

        @pl.when(j >= s)
        def _(s=s):
            key_wait(s)
            scores(j - s, False)

    group_wait(2)
    for h in range(GROUP_HEADS):
        cols = slice(h * PART, (h + 1) * PART)
        inverse = jnp.transpose(jnp.broadcast_to(1.0 / denom[:, cols], (128, PART)))
        heads = c_g[:, h * HEAD_DIM : (h + 1) * HEAD_DIM].astype(jnp.float32)
        for half in range(2):
            lanes = slice(half * 128, (half + 1) * 128)
            cots[cols, lanes] = (heads[:, lanes] * inverse).astype(jnp.bfloat16)

    def dv_copy(s):
        return pltpu.make_async_remote_copy(
            src_ref=dv_out.at[s],
            dst_ref=dv_in.at[s],
            send_sem=dv_send.at[s],
            recv_sem=dv_recv.at[s],
            device_id={"fsdp": (j + 4 - s) % 4 * 4 + g},
            device_id_type=MESH,
        )

    for s in range(1, 4):

        @pl.when(j >= s)
        def _(s=s):
            dv_out[s] = jnp.dot(
                expo[j - s], cots[...], preferred_element_type=jnp.float32
            ).astype(jnp.bfloat16)
            dv_copy(s).start()

    dv_acc[...] = jnp.dot(expo[j], cots[...], preferred_element_type=jnp.float32)

    x_wait((g + 2) % 4, 1)
    x_copy((g + 2) % 4, sibling, 2).start()

    pick(0)

    x_wait(sibling, 0)
    x_wait((sibling + 2) % 4, 2)
    local_copy(3).wait()

    @pl.loop(0, BLOCKS)
    def _(i):
        first = pl.multiple_of(i * 256, 256)
        x_t[pl.ds(first, 256), :] = jnp.transpose(x_g[:, pl.ds(first, 256)])

    for s in range(1, 4):

        @pl.when(j + s < 4)
        def _(s=s):
            dv_copy(s).wait_recv()
            dv_acc[...] += dv_in[s].astype(jnp.float32)

    def gr_copy(s):
        return pltpu.make_async_remote_copy(
            src_ref=gr_out.at[s],
            dst_ref=gr_in.at[s],
            send_sem=gr_send.at[s],
            recv_sem=gr_recv.at[s],
            device_id={"fsdp": (j + s) % 4 * 4 + g},
            device_id_type=MESH,
        )

    dv_low = dv_acc[...].astype(jnp.bfloat16)

    def rows_of(quarter):
        first = pl.multiple_of(quarter * 4 * ROWS, 16)
        return jnp.dot(
            x_t[pl.ds(first, 4 * ROWS), :], dv_low, preferred_element_type=jnp.float32
        )

    for s in range(1, 4):
        gr_out[s] = rows_of((j + s) % 4).astype(jnp.bfloat16)
        gr_copy(s).start()
    gr_acc[...] = rows_of(j)

    pick(1)
    pick(2)

    for s in range(1, 4):
        gr_copy(s).wait_recv()
        gr_acc[...] += gr_in[s].astype(jnp.float32)
    sum_out[...] = gr_acc[...].astype(jnp.bfloat16)

    def own_copy(s):
        peer = (g + s) % 4
        return pltpu.make_async_remote_copy(
            src_ref=sum_out.at[pl.ds(peer * ROWS, ROWS)],
            dst_ref=grad.at[g],
            send_sem=own_send.at[s],
            recv_sem=own_recv.at[s],
            device_id={"fsdp": j * 4 + peer},
            device_id_type=MESH,
        )

    for s in range(1, 4):
        own_copy(s).start()
    grad[g] = sum_out[pl.ds(pl.multiple_of(g * ROWS, 16), ROWS), :]
    for s in range(1, 4):
        slot = grad.at[(g + 4 - s) % 4]
        pltpu.make_async_remote_copy(
            src_ref=slot,
            dst_ref=slot,
            send_sem=own_send.at[s],
            recv_sem=own_recv.at[s],
            device_id={"fsdp": j * 4 + (g + s) % 4},
            device_id_type=MESH,
        ).wait_recv()

    grad_copy = pltpu.make_async_copy(grad, grad_out, out_sem.at[0])
    grad_copy.start()

    for part in range(3):
        to_or_from_sorters(
            part, lambda count: all_of(part, count, deal_send, deal_recv).wait_send()
        )
    for part in range(3):
        to_or_from_sorters(
            part, lambda count: all_of(part, count, pick_send, pick_recv).wait_recv()
        )

    source_copy = pltpu.make_async_copy(source, source_out, out_sem.at[1])
    source_copy.start()

    for s in range(1, 4):
        for kind in range(3):
            group_copy(kind, s).wait_send()

        @pl.when(j + s < 4)
        def _(s=s):
            key_copy(s).wait_send()

        @pl.when(j >= s)
        def _(s=s):
            dv_copy(s).wait_send()

        gr_copy(s).wait_send()
        own_copy(s).wait_send()
    x_copy(g, sibling, 0).wait_send()
    x_copy(g, (g + 2) % 4, 1).wait_send()
    x_copy((g + 2) % 4, sibling, 2).wait_send()

    for part in range(3):
        sorts(
            me, part, lambda: all_of(part, MEMBERS - 1, pick_send, pick_recv).wait_send()
        )

    grad_copy.wait()
    source_copy.wait()


def adam_kernel(grad, source, new_w, new_m, new_v):
    for band in range(8):
        cols = slice(band * 128, (band + 1) * 128)
        lanes = slice(band % 2 * 128, band % 2 * 128 + 128)
        gradient = grad[band // 2, :, lanes].astype(jnp.float32)
        old_w = source[band, 0:ROWS].astype(jnp.float32)
        old_m = source[band, ROWS : 2 * ROWS].astype(jnp.float32)
        old_v = source[band, 2 * ROWS : 3 * ROWS].astype(jnp.float32)
        first = beta_one * old_m + (1.0 - beta_one) * gradient
        second = beta_two * old_v + (1.0 - beta_two) * gradient * gradient
        first_hat = first * (1.0 / (1.0 - beta_one**adam_step))
        second_hat = second * (1.0 / (1.0 - beta_two**adam_step))
        update = first_hat / (jnp.sqrt(second_hat) + adam_eps) + decay_rate * old_w
        new_w[:, cols] = (old_w - learning_rate * update).astype(jnp.bfloat16)
        new_m[:, cols] = first
        new_v[:, cols] = second


def local(inputs, queries, keys, cotangent, winners, weights, first_moment, second_moment):
    f32, bf16 = jnp.float32, jnp.bfloat16
    vmem = pl.BlockSpec(memory_space=pltpu.VMEM)
    hbm = pl.BlockSpec(memory_space=pltpu.HBM)
    dma = pltpu.SemaphoreType.DMA
    grad, source = pl.pallas_call(
        kernel,
        out_shape=(
            jax.ShapeDtypeStruct((4, ROWS, HEAD_DIM), bf16),
            jax.ShapeDtypeStruct((8, 3 * ROWS, 128), bf16),
        ),
        in_specs=[pl.BlockSpec(memory_space=pltpu.SMEM)] + [hbm] * 7,
        out_specs=(hbm, hbm),
        scratch_shapes=[
            pltpu.VMEM((QUARTERS, PART, HEAD_DIM), bf16),
            pltpu.VMEM((PART, GROUP_HEADS * HEAD_DIM), bf16),
            pltpu.VMEM((PART, GROUP_HEADS * HEAD_DIM), bf16),
            pltpu.VMEM((PART, FEAT), bf16),
            pltpu.VMEM((FEAT, PART), bf16),
            pltpu.VMEM((QUARTERS, PART, GROUP_HEADS * PART), bf16),
            pltpu.VMEM((1, GROUP_HEADS * PART), f32),
            pltpu.VMEM((GROUP_HEADS * PART, HEAD_DIM), bf16),
            pltpu.VMEM((PART, HEAD_DIM), f32),
            pltpu.VMEM((4, PART, HEAD_DIM), bf16),
            pltpu.VMEM((4, PART, HEAD_DIM), bf16),
            pltpu.VMEM((4 * ROWS, HEAD_DIM), f32),
            pltpu.VMEM((4, 4 * ROWS, HEAD_DIM), bf16),
            pltpu.VMEM((4, 4 * ROWS, HEAD_DIM), bf16),
            pltpu.VMEM((4 * ROWS, HEAD_DIM), bf16),
            pltpu.VMEM((4, ROWS, HEAD_DIM), bf16),
            pltpu.VMEM((ROWS, KVW), bf16),
            pltpu.VMEM((ROWS, KVW), f32),
            pltpu.VMEM((ROWS, KVW), f32),
            pltpu.VMEM((8, 3 * ROWS, 128), bf16),
            pltpu.VMEM((MEMBERS, 48, 128), bf16),
            pltpu.VMEM((MEMBERS, 32, 128), bf16),
            pltpu.VMEM((MEMBERS, 16, 128), bf16),
            pltpu.VMEM((MEMBERS, 48, 128), bf16),
            pltpu.VMEM((MEMBERS, 32, 128), bf16),
            pltpu.VMEM((MEMBERS, 16, 128), bf16),
            pltpu.VMEM((8, 3 * ROWS, 128), bf16),
            dma((4,)),
            dma((3,)),
            dma((2,)),
            dma((4, 4)),
            dma((4, 4)),
            dma((4,)),
            dma((4,)),
            dma((4,)),
            dma((4,)),
            dma((4,)),
            dma((4,)),
            dma((4,)),
            dma((4,)),
            dma((4,)),
            dma((4,)),
            dma((3,)),
            dma((3,)),
            dma((3,)),
            dma((3,)),
        ],
        compiler_params=pltpu.CompilerParams(
            collective_id=0, has_side_effects=True, vmem_limit_bytes=VMEM_LIMIT
        ),
        cost_estimate=pl.CostEstimate(
            flops=3_000_000_000, bytes_accessed=6_000_000, transcendentals=4_000_000
        ),
    )(
        winners, inputs[0], queries[0], keys[0], cotangent[0],
        weights[0], first_moment[0], second_moment[0],
    )
    outs = pl.pallas_call(
        adam_kernel,
        out_shape=(
            jax.ShapeDtypeStruct((ROWS, KVW), bf16),
            jax.ShapeDtypeStruct((ROWS, KVW), f32),
            jax.ShapeDtypeStruct((ROWS, KVW), f32),
        ),
        in_specs=[vmem, vmem],
        out_specs=(vmem, vmem, vmem),
        compiler_params=pltpu.CompilerParams(vmem_limit_bytes=VMEM_LIMIT),
    )(grad, source)
    return tuple(out[None] for out in outs)


def solution(mesh):
    rows = P("member", "fsdp", None)
    return jax.shard_map(
        local,
        mesh=mesh,
        in_specs=(rows, rows, rows, rows, P(), rows, rows, rows),
        out_specs=(rows, rows, rows),
        check_vma=False,
    )
```

```python
import jax
import jax.numpy as jnp
from jax import lax
from jax.experimental import pallas as pl
from jax.experimental.pallas import tpu as pltpu
from jax.sharding import PartitionSpec as P

MEMBERS = 32
KV_HEADS = 4
QUARTERS = 4
HEAD_DIM = 256
GROUP_HEADS = 2
TOK = 128
FEAT = 1792
ROWS = 112
KVW = 1024
PART = QUARTERS * TOK
PIECE = 80
BLOCKS = 7

beta_one = 0.9
beta_two = 0.999
learning_rate = 0.001
decay_rate = 0.1
adam_eps = 1e-08
adam_step = 200
soft_cap = 50.0

VMEM_LIMIT = 60 * 1024 * 1024

MESH = pl.DeviceIdType.MESH


def kernel(
    winners, x_in, q_in, k_in, c_in, w_in, m_in, v_in,
    grad_out, source_out,
    k_all, q_g, c_g, x_g, x_t, expo, denom, cots,
    dv_acc, dv_out, dv_in, gr_acc, gr_out, gr_in, sum_out, grad,
    w_own, m_own, v_own, state, dealt_0, dealt_1, dealt_2, picked_0, picked_1, picked_2, source,
    loc_sem, own_sem, out_sem, grp_send, grp_recv, key_send, key_recv, dv_send, dv_recv,
    gr_send, gr_recv, own_send, own_recv, deal_send, deal_recv, pick_send, pick_recv,
):
    me = lax.axis_index("member")
    mine = lax.axis_index("fsdp")
    g = mine // QUARTERS
    j = mine % QUARTERS

    def at(quarter, head):
        return {"fsdp": head * QUARTERS + quarter}

    state_copies = [
        pltpu.make_async_copy(src, dst, own_sem.at[i])
        for i, (src, dst) in enumerate(((w_in, w_own), (m_in, m_own), (v_in, v_own)))
    ]
    for copy in state_copies:
        copy.start()

    barrier = pltpu.get_barrier_semaphore()
    for s in range(1, 4):
        pl.semaphore_signal(
            barrier, inc=1, device_id=at(j, (g + s) % 4), device_id_type=MESH
        )
        pl.semaphore_signal(
            barrier, inc=1, device_id=at((j + s) % 4, g), device_id_type=MESH
        )

    @pl.loop(1, MEMBERS)
    def _(s):
        pl.semaphore_signal(
            barrier, inc=1, device_id={"member": (me + s) % MEMBERS}, device_id_type=MESH
        )

    def own_slot(kind, owner):
        rows = pl.ds(owner * TOK, TOK)
        return (k_all.at[j, rows], q_g.at[rows], c_g.at[rows], x_g.at[rows])[kind]

    def own_slice(kind, head):
        if kind == 0:
            return k_in.at[:, pl.ds(head * HEAD_DIM, HEAD_DIM)]
        if kind == 3:
            return x_in
        wide = GROUP_HEADS * HEAD_DIM
        return (q_in, c_in)[kind - 1].at[:, pl.ds(head * wide, wide)]

    def group_copy(kind, s):
        peer = (g + s) % 4
        return pltpu.make_async_remote_copy(
            src_ref=own_slice(kind, peer),
            dst_ref=own_slot(kind, g),
            send_sem=grp_send.at[kind, s],
            recv_sem=grp_recv.at[kind, s],
            device_id=at(j, peer),
            device_id_type=MESH,
        )

    def group_wait(kind):
        for s in range(1, 4):
            slot = own_slot(kind, (g + 4 - s) % 4)
            pltpu.make_async_remote_copy(
                src_ref=slot,
                dst_ref=slot,
                send_sem=grp_send.at[kind, s],
                recv_sem=grp_recv.at[kind, s],
                device_id=at(j, (g + s) % 4),
                device_id_type=MESH,
            ).wait_recv()
        local_copy(kind).wait()

    def local_copy(kind):
        return pltpu.make_async_copy(own_slice(kind, g), own_slot(kind, g), loc_sem.at[kind])

    for kind in range(4):
        local_copy(kind).start()

    for copy in state_copies:
        copy.wait()
    for band in range(8):
        cols = slice(band * 128, (band + 1) * 128)
        state[band, 0:ROWS] = w_own[:, cols]
        state[band, ROWS : 2 * ROWS] = m_own[:, cols].astype(jnp.bfloat16)
        state[band, 2 * ROWS : 3 * ROWS] = v_own[:, cols].astype(jnp.bfloat16)

    pl.semaphore_wait(barrier, 6 + MEMBERS - 1)

    for kind in range(3):
        for s in range(1, 4):
            group_copy(kind, s).start()

    core = mine % 2
    starts, sizes = (0, 48, 80), (48, 32, 16)
    dealt, picked = (dealt_0, dealt_1, dealt_2), (picked_0, picked_1, picked_2)

    def extra(member):
        return (member + 2 * core) % 4 == 1

    def sorts(member, part, action):
        if part < 2:
            action()
        else:
            pl.when(extra(member))(action)

    def place(ref, member, part):
        first = member % 4 * PIECE + starts[part] if part < 2 else 4 * PIECE
        return ref.at[member // 4, pl.ds(first, sizes[part])]

    def deal_copy(s, part):
        peer = (me + s) % MEMBERS
        return pltpu.make_async_remote_copy(
            src_ref=place(state, peer, part),
            dst_ref=dealt[part].at[me],
            send_sem=deal_send.at[part],
            recv_sem=deal_recv.at[part],
            device_id={"member": peer},
            device_id_type=MESH,
        )

    def all_of(part, count, send_sem, recv_sem):
        ref = dealt[part].at[pl.ds(0, count)]
        return pltpu.make_async_remote_copy(
            src_ref=ref,
            dst_ref=ref,
            send_sem=send_sem.at[part],
            recv_sem=recv_sem.at[part],
            device_id={"member": (me + 1) % MEMBERS},
            device_id_type=MESH,
        )

    def to_or_from_sorters(part, wait):
        if part < 2:
            wait(MEMBERS - 1)
        else:
            pl.when(extra(me))(lambda: wait(MEMBERS // 4 - 1))
            pl.when(jnp.logical_not(extra(me)))(lambda: wait(MEMBERS // 4))

    for part in range(3):

        @pl.loop(1, MEMBERS)
        def _(s):
            sorts((me + s) % MEMBERS, part, lambda: deal_copy(s, part).start())

    for s in range(1, 4):
        group_copy(3, s).start()

    def keep(part):
        dealt[part][me] = place(state, me, part)[...]

    for part in range(3):
        sorts(me, part, lambda: keep(part))

    def pick_copy(s, part):
        peer = (me + s) % MEMBERS
        return pltpu.make_async_remote_copy(
            src_ref=picked[part].at[s],
            dst_ref=place(source, me, part),
            send_sem=pick_send.at[part],
            recv_sem=pick_recv.at[part],
            device_id={"member": peer},
            device_id_type=MESH,
        )

    def pick(part):
        def action():
            all_of(part, MEMBERS - 1, deal_send, deal_recv).wait_recv()

            @pl.loop(1, MEMBERS)
            def _(s):
                picked[part][s] = dealt[part][winners[(me + s) % MEMBERS]]
                pick_copy(s, part).start()

            place(source, me, part)[...] = dealt[part][winners[me]]

        sorts(me, part, action)

    def key_copy(s):
        return pltpu.make_async_remote_copy(
            src_ref=k_all.at[j],
            dst_ref=k_all.at[j],
            send_sem=key_send.at[s],
            recv_sem=key_recv.at[s],
            device_id=at((j + s) % 4, g),
            device_id_type=MESH,
        )

    def key_wait(s):
        slot = k_all.at[(j + 4 - s) % 4]
        pltpu.make_async_remote_copy(
            src_ref=slot,
            dst_ref=slot,
            send_sem=key_send.at[s],
            recv_sem=key_recv.at[s],
            device_id=at((j + s) % 4, g),
            device_id_type=MESH,
        ).wait_recv()

    group_wait(0)
    for s in range(1, 4):
        key_copy(s).start()

    group_wait(1)
    denom[...] = jnp.zeros_like(denom)

    def scores(chunk):
        later = jnp.where(chunk > j, TOK, jnp.where(chunk < j, -TOK, 0))
        for i in range(4):
            first = i * TOK
            key_block = k_all[chunk, first : first + TOK, :]
            for h in range(GROUP_HEADS):
                raw = lax.dot_general(
                    key_block,
                    q_g[first:PART, h * HEAD_DIM : (h + 1) * HEAD_DIM],
                    (((1,), (1,)), ((), ())),
                    preferred_element_type=jnp.float32,
                )
                e = jnp.exp(soft_cap * jnp.tanh(raw * (HEAD_DIM**-0.5 / soft_cap)))
                u = lax.broadcasted_iota(jnp.int32, raw.shape, 0)
                t = lax.broadcasted_iota(jnp.int32, raw.shape, 1)
                e = jnp.where((u + later <= t) | (t >= TOK), e, 0.0)
                cols = slice(h * PART + first, (h + 1) * PART)
                expo[chunk, first : first + TOK, cols] = e.astype(jnp.bfloat16)
                denom[:, cols] += jnp.sum(e, axis=0, keepdims=True)

    scores(j)

    @pl.loop(1, 4)
    def _(s):
        key_wait(s)
        scores((j + 4 - s) % 4)

    group_wait(2)
    for h in range(GROUP_HEADS):
        cols = slice(h * PART, (h + 1) * PART)
        inverse = jnp.transpose(jnp.broadcast_to(1.0 / denom[:, cols], (128, PART)))
        heads = c_g[:, h * HEAD_DIM : (h + 1) * HEAD_DIM].astype(jnp.float32)
        for half in range(2):
            lanes = slice(half * 128, (half + 1) * 128)
            cots[cols, lanes] = (heads[:, lanes] * inverse).astype(jnp.bfloat16)

    def dv_copy(s):
        return pltpu.make_async_remote_copy(
            src_ref=dv_out.at[s],
            dst_ref=dv_in.at[s],
            send_sem=dv_send.at[s],
            recv_sem=dv_recv.at[s],
            device_id=at((j + 4 - s) % 4, g),
            device_id_type=MESH,
        )

    def dv_rows(chunk, i):
        first = i * TOK
        total = None
        for h in range(GROUP_HEADS):
            cols = slice(h * PART + first, (h + 1) * PART)
            term = jnp.dot(
                expo[chunk, first : first + TOK, cols],
                cots[cols, :],
                preferred_element_type=jnp.float32,
            )
            total = term if total is None else total + term
        return total

    @pl.loop(1, 4)
    def _(s):
        for i in range(4):
            dv_out[s, i * TOK : (i + 1) * TOK] = dv_rows((j + 4 - s) % 4, i).astype(jnp.bfloat16)
        dv_copy(s).start()

    for i in range(4):
        dv_acc[i * TOK : (i + 1) * TOK] = dv_rows(j, i)

    pick(0)

    group_wait(3)

    @pl.loop(0, BLOCKS)
    def _(i):
        first = pl.multiple_of(i * 256, 256)
        x_t[pl.ds(first, 256), :] = jnp.transpose(x_g[:, pl.ds(first, 256)])

    for s in range(1, 4):
        dv_copy(s).wait_recv()
        dv_acc[...] += dv_in[s].astype(jnp.float32)

    def gr_copy(s):
        return pltpu.make_async_remote_copy(
            src_ref=gr_out.at[s],
            dst_ref=gr_in.at[s],
            send_sem=gr_send.at[s],
            recv_sem=gr_recv.at[s],
            device_id=at((j + s) % 4, g),
            device_id_type=MESH,
        )

    dv_low = dv_acc[...].astype(jnp.bfloat16)

    def rows_of(quarter, i):
        first = pl.multiple_of((i * QUARTERS + quarter) * ROWS, 16)
        return jnp.dot(x_t[pl.ds(first, ROWS), :], dv_low, preferred_element_type=jnp.float32)

    for s in range(1, 4):
        for i in range(4):
            gr_out[s, i * ROWS : (i + 1) * ROWS] = rows_of((j + s) % 4, i).astype(jnp.bfloat16)
        gr_copy(s).start()
    for i in range(4):
        gr_acc[i * ROWS : (i + 1) * ROWS] = rows_of(j, i)

    pick(1)
    pick(2)

    for s in range(1, 4):
        gr_copy(s).wait_recv()
        gr_acc[...] += gr_in[s].astype(jnp.float32)
    sum_out[...] = gr_acc[...].astype(jnp.bfloat16)

    def own_copy(s):
        peer = (g + s) % 4
        return pltpu.make_async_remote_copy(
            src_ref=sum_out.at[pl.ds(peer * ROWS, ROWS)],
            dst_ref=grad.at[g],
            send_sem=own_send.at[s],
            recv_sem=own_recv.at[s],
            device_id=at(j, peer),
            device_id_type=MESH,
        )

    for s in range(1, 4):
        own_copy(s).start()
    grad[g] = sum_out[pl.ds(pl.multiple_of(g * ROWS, 16), ROWS), :]
    for s in range(1, 4):
        slot = grad.at[(g + 4 - s) % 4]
        pltpu.make_async_remote_copy(
            src_ref=slot,
            dst_ref=slot,
            send_sem=own_send.at[s],
            recv_sem=own_recv.at[s],
            device_id=at(j, (g + s) % 4),
            device_id_type=MESH,
        ).wait_recv()

    grad_copy = pltpu.make_async_copy(grad, grad_out, out_sem.at[0])
    grad_copy.start()

    for part in range(3):
        to_or_from_sorters(
            part, lambda count: all_of(part, count, deal_send, deal_recv).wait_send()
        )
    for part in range(3):
        to_or_from_sorters(
            part, lambda count: all_of(part, count, pick_send, pick_recv).wait_recv()
        )

    source_copy = pltpu.make_async_copy(source, source_out, out_sem.at[1])
    source_copy.start()

    for s in range(1, 4):
        for kind in range(4):
            group_copy(kind, s).wait_send()

        key_copy(s).wait_send()
        dv_copy(s).wait_send()
        gr_copy(s).wait_send()
        own_copy(s).wait_send()

    for part in range(3):
        sorts(
            me, part, lambda: all_of(part, MEMBERS - 1, pick_send, pick_recv).wait_send()
        )

    grad_copy.wait()
    source_copy.wait()


def adam_kernel(grad, source, new_w, new_m, new_v):
    for band in range(8):
        cols = slice(band * 128, (band + 1) * 128)
        lanes = slice(band % 2 * 128, band % 2 * 128 + 128)
        gradient = grad[band // 2, :, lanes].astype(jnp.float32)
        old_w = source[band, 0:ROWS].astype(jnp.float32)
        old_m = source[band, ROWS : 2 * ROWS].astype(jnp.float32)
        old_v = source[band, 2 * ROWS : 3 * ROWS].astype(jnp.float32)
        first = beta_one * old_m + (1.0 - beta_one) * gradient
        second = beta_two * old_v + (1.0 - beta_two) * gradient * gradient
        first_hat = first * (1.0 / (1.0 - beta_one**adam_step))
        second_hat = second * (1.0 / (1.0 - beta_two**adam_step))
        update = first_hat / (jnp.sqrt(second_hat) + adam_eps) + decay_rate * old_w
        new_w[:, cols] = (old_w - learning_rate * update).astype(jnp.bfloat16)
        new_m[:, cols] = first
        new_v[:, cols] = second


def local(inputs, queries, keys, cotangent, winners, weights, first_moment, second_moment):
    f32, bf16 = jnp.float32, jnp.bfloat16
    vmem = pl.BlockSpec(memory_space=pltpu.VMEM)
    hbm = pl.BlockSpec(memory_space=pltpu.HBM)
    dma = pltpu.SemaphoreType.DMA
    grad, source = pl.pallas_call(
        kernel,
        out_shape=(
            jax.ShapeDtypeStruct((4, ROWS, HEAD_DIM), bf16),
            jax.ShapeDtypeStruct((8, 3 * ROWS, 128), bf16),
        ),
        in_specs=[pl.BlockSpec(memory_space=pltpu.SMEM)] + [hbm] * 7,
        out_specs=(hbm, hbm),
        scratch_shapes=[
            pltpu.VMEM((QUARTERS, PART, HEAD_DIM), bf16),
            pltpu.VMEM((PART, GROUP_HEADS * HEAD_DIM), bf16),
            pltpu.VMEM((PART, GROUP_HEADS * HEAD_DIM), bf16),
            pltpu.VMEM((PART, FEAT), bf16),
            pltpu.VMEM((FEAT, PART), bf16),
            pltpu.VMEM((QUARTERS, PART, GROUP_HEADS * PART), bf16),
            pltpu.VMEM((1, GROUP_HEADS * PART), f32),
            pltpu.VMEM((GROUP_HEADS * PART, HEAD_DIM), bf16),
            pltpu.VMEM((PART, HEAD_DIM), f32),
            pltpu.VMEM((4, PART, HEAD_DIM), bf16),
            pltpu.VMEM((4, PART, HEAD_DIM), bf16),
            pltpu.VMEM((4 * ROWS, HEAD_DIM), f32),
            pltpu.VMEM((4, 4 * ROWS, HEAD_DIM), bf16),
            pltpu.VMEM((4, 4 * ROWS, HEAD_DIM), bf16),
            pltpu.VMEM((4 * ROWS, HEAD_DIM), bf16),
            pltpu.VMEM((4, ROWS, HEAD_DIM), bf16),
            pltpu.VMEM((ROWS, KVW), bf16),
            pltpu.VMEM((ROWS, KVW), f32),
            pltpu.VMEM((ROWS, KVW), f32),
            pltpu.VMEM((8, 3 * ROWS, 128), bf16),
            pltpu.VMEM((MEMBERS, 48, 128), bf16),
            pltpu.VMEM((MEMBERS, 32, 128), bf16),
            pltpu.VMEM((MEMBERS, 16, 128), bf16),
            pltpu.VMEM((MEMBERS, 48, 128), bf16),
            pltpu.VMEM((MEMBERS, 32, 128), bf16),
            pltpu.VMEM((MEMBERS, 16, 128), bf16),
            pltpu.VMEM((8, 3 * ROWS, 128), bf16),
            dma((4,)),
            dma((3,)),
            dma((2,)),
            dma((4, 4)),
            dma((4, 4)),
            dma((4,)),
            dma((4,)),
            dma((4,)),
            dma((4,)),
            dma((4,)),
            dma((4,)),
            dma((4,)),
            dma((4,)),
            dma((3,)),
            dma((3,)),
            dma((3,)),
            dma((3,)),
        ],
        compiler_params=pltpu.CompilerParams(
            collective_id=0, has_side_effects=True, vmem_limit_bytes=VMEM_LIMIT
        ),
        cost_estimate=pl.CostEstimate(
            flops=3_000_000_000, bytes_accessed=6_000_000, transcendentals=4_000_000
        ),
    )(
        winners, inputs[0], queries[0], keys[0], cotangent[0],
        weights[0], first_moment[0], second_moment[0],
    )
    outs = pl.pallas_call(
        adam_kernel,
        out_shape=(
            jax.ShapeDtypeStruct((ROWS, KVW), bf16),
            jax.ShapeDtypeStruct((ROWS, KVW), f32),
            jax.ShapeDtypeStruct((ROWS, KVW), f32),
        ),
        in_specs=[vmem, vmem],
        out_specs=(vmem, vmem, vmem),
        compiler_params=pltpu.CompilerParams(vmem_limit_bytes=VMEM_LIMIT),
    )(grad, source)
    return tuple(out[None] for out in outs)


def solution(mesh):
    rows = P("member", "fsdp", None)
    return jax.shard_map(
        local,
        mesh=mesh,
        in_specs=(rows, rows, rows, rows, P(), rows, rows, rows),
        out_specs=(rows, rows, rows),
        check_vma=False,
    )
```

```python
import jax
import jax.numpy as jnp
from jax import lax
from jax.experimental import pallas as pl
from jax.experimental.pallas import tpu as pltpu
from jax.sharding import PartitionSpec as P

MEMBERS = 32
KV_HEADS = 4
QUARTERS = 4
HEAD_DIM = 256
GROUP_HEADS = 2
TOK = 128
FEAT = 1792
X_HALF = 896
ROWS = 112
KVW = 1024
PART = QUARTERS * TOK
PIECE = 80
RING = 16
HALF = 8
SLOTS = 5
BLOCKS = 7

beta_one = 0.9
beta_two = 0.999
learning_rate = 0.001
decay_rate = 0.1
adam_eps = 1e-08
adam_step = 200
soft_cap = 50.0

VMEM_LIMIT = 60 * 1024 * 1024

MESH = pl.DeviceIdType.MESH


def kernel(
    winners, x_in, q_in, k_in, c_in, w_in, m_in, v_in,
    grad_out, source_out, flag_out,
    k_all, q_g, c_g, x_g, x_t, expo, denom, cots,
    dv_acc, dv_out, dv_in, gr_acc, gr_out, gr_in, sum_out, grad,
    w_own, m_own, v_own, state, source, table_v, table_s,
    loc_sem, own_sem, out_sem, grp_send, grp_recv, key_send, key_recv, dv_send, dv_recv,
    gr_send, gr_recv, own_send, own_recv, x_send, x_recv, deal_send, deal_recv, swap_send, swap_recv,
    pick_send, pick_recv, *parts,
):
    me = lax.axis_index("member")
    mine = lax.axis_index("fsdp")
    dealt, swap_out, swap_in, sent = (
        [(parts[8 * part + 2 * kind], parts[8 * part + 2 * kind + 1]) for part in range(3)]
        for kind in range(4)
    )
    both = parts[24:27]
    g = mine // QUARTERS
    j = mine % QUARTERS

    def at(quarter, head):
        return {"fsdp": head * QUARTERS + quarter}

    state_copies = [
        pltpu.make_async_copy(src, dst, own_sem.at[i])
        for i, (src, dst) in enumerate(((w_in, w_own), (m_in, m_own), (v_in, v_own)))
    ]
    for copy in state_copies:
        copy.start()

    barrier = pltpu.get_barrier_semaphore()
    for s in range(1, 4):
        pl.semaphore_signal(
            barrier, inc=1, device_id=at(j, (g + s) % 4), device_id_type=MESH
        )
        pl.semaphore_signal(
            barrier, inc=1, device_id=at((j + s) % 4, g), device_id_type=MESH
        )

    def greet(offset, row):
        pl.semaphore_signal(
            barrier,
            inc=1,
            device_id={
                "member": (me // RING + row) % 2 * RING + (me + RING + offset) % RING
            },
            device_id_type=MESH,
        )

    @pl.loop(1, 6)
    def _(s):
        for row in range(2):
            greet(s, row)
            greet(-s, row)

    greet(0, 1)

    def own_slot(kind, owner):
        rows = pl.ds(owner * TOK, TOK)
        return (k_all.at[j, rows], q_g.at[rows], c_g.at[rows], x_g.at[rows])[kind]

    def own_slice(kind, head):
        if kind == 0:
            return k_in.at[:, pl.ds(head * HEAD_DIM, HEAD_DIM)]
        if kind == 3:
            return x_in
        wide = GROUP_HEADS * HEAD_DIM
        return (q_in, c_in)[kind - 1].at[:, pl.ds(head * wide, wide)]

    def group_copy(kind, s):
        peer = (g + s) % 4
        return pltpu.make_async_remote_copy(
            src_ref=own_slice(kind, peer),
            dst_ref=own_slot(kind, g),
            send_sem=grp_send.at[kind, s],
            recv_sem=grp_recv.at[kind, s],
            device_id=at(j, peer),
            device_id_type=MESH,
        )

    def group_wait(kind):
        for s in range(1, 4):
            slot = own_slot(kind, (g + 4 - s) % 4)
            pltpu.make_async_remote_copy(
                src_ref=slot,
                dst_ref=slot,
                send_sem=grp_send.at[kind, s],
                recv_sem=grp_recv.at[kind, s],
                device_id=at(j, (g + s) % 4),
                device_id_type=MESH,
            ).wait_recv()
        local_copy(kind).wait()

    def local_copy(kind):
        return pltpu.make_async_copy(own_slice(kind, g), own_slot(kind, g), loc_sem.at[kind])

    for kind in range(4):
        local_copy(kind).start()

    for copy in state_copies:
        copy.wait()
    for band in range(8):
        cols = slice(band * 128, (band + 1) * 128)
        state[band, 0:ROWS] = w_own[:, cols]
        state[band, ROWS : 2 * ROWS] = m_own[:, cols].astype(jnp.bfloat16)
        state[band, 2 * ROWS : 3 * ROWS] = v_own[:, cols].astype(jnp.bfloat16)

    pl.semaphore_wait(barrier, 6 + 21)

    for kind in range(3):
        for s in range(1, 4):
            group_copy(kind, s).start()

    core = mine % 2
    y = me // RING
    z = me % RING
    starts, sizes = (0, 48, 80), (48, 32, 16)
    cuts = ((z + RING - 5) % RING, (z + RING - 10) % RING)
    reach = (5, 2)

    def special(r):
        return (r + 2 * core) % 4 == 1

    def has(part, r, action):
        if part < 2:
            action()
        else:
            pl.when(special(r))(action)

    def place(ref, r, part, row=None):
        piece = (y if row is None else row) * RING + r
        first = piece % 4 * PIECE + starts[part] if part < 2 else 4 * PIECE
        return ref.at[piece // 4, pl.ds(first, sizes[part])]

    def bulk(part, count, send_sem, recv_sem):
        ref = sent[part][0].at[pl.ds(0, 15)] if count == 15 else both[part].at[pl.ds(0, count)]
        return pltpu.make_async_remote_copy(
            src_ref=ref,
            dst_ref=ref,
            send_sem=send_sem,
            recv_sem=recv_sem,
            device_id={"member": (me + 1) % MEMBERS},
            device_id_type=MESH,
        )

    def in_all(part, wait):
        if part < 2:
            wait(30)
        else:
            either = special(cuts[0]) | special(cuts[1])
            pl.when(either)(lambda: wait(7))
            pl.when(jnp.logical_not(either))(lambda: wait(8))

    def deal(part):
        @pl.loop(0, HALF)
        def _(d):
            for role in range(2):
                r = (z + RING - HALF * role - d) % RING
                for row in range(2):

                    def start(role=role, row=row, r=r):
                        pltpu.make_async_remote_copy(
                            src_ref=place(state, r, part, row),
                            dst_ref=dealt[part][role].at[y * HALF + d],
                            send_sem=deal_send.at[part],
                            recv_sem=deal_recv.at[part, role],
                            device_id={
                                "member": row * RING + (z + RING + reach[role] - d) % RING
                            },
                            device_id_type=MESH,
                        ).start()

                    other = (d != reach[role]) | (y != row)
                    pl.when(other if part < 2 else other & special(r))(start)

        for role in range(2):

            def keep(role=role):
                dealt[part][role][y * HALF + reach[role]] = place(state, cuts[role], part)[...]

            has(part, cuts[role], keep)

    def slot(member, role):
        return member // RING * HALF + (member % RING + RING - cuts[role]) % HALF

    def swap_copy(part, role):
        partner = (z + 5) % RING if role == 0 else (z + RING - 5) % RING
        return pltpu.make_async_remote_copy(
            src_ref=swap_out[part][role],
            dst_ref=swap_in[part][1 - role],
            send_sem=swap_send.at[part, role],
            recv_sem=swap_recv.at[part, 1 - role],
            device_id={"member": y * RING + partner},
            device_id_type=MESH,
        )

    def swap(part):
        for role in range(2):

            def action(role=role):
                bulk(part, 15, deal_send.at[part], deal_recv.at[part, role]).wait_recv()
                for k in range(SLOTS):
                    swap_out[part][role][k] = dealt[part][role][slot(table_s[2 * role, k], role)]
                swap_copy(part, role).start()

            has(part, cuts[role], action)

    def serve(part):
        for role in range(2):

            def action(role=role):
                swap_copy(part, 1 - role).wait_recv()

                @pl.loop(0, HALF)
                def _(d):
                    for row in range(2):
                        member = row * RING + (z + RING - reach[role] + d) % RING
                        winner = winners[member]
                        inside = (winner % RING + RING - cuts[role]) % RING // HALF == role
                        near = dealt[part][role][slot(winner, role)]
                        rank = jnp.minimum(table_s[2 * role + 1, winner], SLOTS - 1)
                        far = swap_in[part][role][rank]
                        sent[part][role][row * HALF + d] = jnp.where(inside, near, far)

                        def start(row=row, member=member):
                            pltpu.make_async_remote_copy(
                                src_ref=sent[part][role].at[row * HALF + d],
                                dst_ref=place(source, cuts[role], part),
                                send_sem=pick_send.at[part],
                                recv_sem=pick_recv.at[part],
                                device_id={"member": member},
                                device_id_type=MESH,
                            ).start()

                        pl.when((d != reach[role]) | (y != row))(start)

                place(source, cuts[role], part)[...] = sent[part][role][y * HALF + reach[role]]

            has(part, cuts[role], action)

    for part in range(3):
        deal(part)

    right, left = (g + 1) % 4, (g + 3) % 4
    routes = ((0, g, right), (0, g, left), (1, g, left), (1, g, right), (0, left, right), (1, right, left))
    x_from = (left, right, right, left, left, right)
    x_owner = (left, right, right, left, (g + 2) % 4, (g + 2) % 4)

    def x_slot(owner, half):
        return x_g.at[pl.ds(owner * TOK, TOK), pl.ds(half * X_HALF, X_HALF)]

    def x_copy(route):
        half, owner, peer = routes[route]
        slot = x_slot(owner, half)
        return pltpu.make_async_remote_copy(
            src_ref=slot if route > 3 else x_in.at[:, pl.ds(half * X_HALF, X_HALF)],
            dst_ref=slot,
            send_sem=x_send.at[route],
            recv_sem=x_recv.at[route],
            device_id=at(j, peer),
            device_id_type=MESH,
        )

    def x_wait(route):
        slot = x_slot(x_owner[route], routes[route][0])
        pltpu.make_async_remote_copy(
            src_ref=slot,
            dst_ref=slot,
            send_sem=x_send.at[route],
            recv_sem=x_recv.at[route],
            device_id=at(j, x_from[route]),
            device_id_type=MESH,
        ).wait_recv()

    for route in range(4):
        x_copy(route).start()

    shape = (MEMBERS, 128)
    sub = lax.broadcasted_iota(jnp.int32, shape, 0)
    lane = lax.broadcasted_iota(jnp.int32, shape, 1)
    by_sub = jnp.zeros(shape, jnp.int32)
    by_lane = jnp.full(shape, -1, jnp.int32)
    for b in range(MEMBERS):
        by_sub = jnp.where(sub == b, winners[b], by_sub)
        by_lane = jnp.where(lane == b, winners[b], by_lane)
    one, none = jnp.ones(shape, jnp.int32), jnp.zeros(shape, jnp.int32)
    takes = jnp.where(by_lane == sub, one, none)
    taken = jnp.where(by_sub == lane, one, none)

    def inside_of(index, r, role):
        return jnp.where((index % RING + RING - r) % RING // HALF == role, one, none)

    def needed_by(r, role):
        in_sub, in_lane = inside_of(sub, r, role), inside_of(lane, r, role)
        out_sub = in_sub * jnp.max(takes * (1 - in_lane), axis=1, keepdims=True)
        return in_sub, in_lane, out_sub

    for role in range(2):
        in_sub, in_lane, out_sub = needed_by(cuts[role], role)
        out_lane = in_lane * jnp.max(taken * (1 - in_sub), axis=0, keepdims=True)
        rank = jnp.sum(jnp.where(lane < sub, out_lane, none), axis=1, keepdims=True)
        chosen = jnp.where(rank == lane, out_sub * sub, none)
        table_v[2 * role : 2 * role + 1, :] = jnp.sum(chosen, axis=0, keepdims=True)
        in_need = (1 - in_sub) * jnp.max(takes * in_lane, axis=1, keepdims=True)
        table_v[2 * role + 1 : 2 * role + 2, :] = jnp.sum(
            jnp.where(sub < lane, in_need, none), axis=0, keepdims=True
        )
    table_copy = pltpu.make_async_copy(table_v, table_s, out_sem.at[2])
    table_copy.start()

    most = jnp.zeros((1, 128), jnp.int32)
    for r in range(RING):
        most = jnp.maximum(most, jnp.sum(needed_by(r, 0)[2], axis=0, keepdims=True))
    flag_out[0] = jnp.max(jnp.where(most > SLOTS, 1, 0))
    table_copy.wait()

    def key_copy(s):
        return pltpu.make_async_remote_copy(
            src_ref=k_all.at[j],
            dst_ref=k_all.at[j],
            send_sem=key_send.at[s],
            recv_sem=key_recv.at[s],
            device_id=at((j + s) % 4, g),
            device_id_type=MESH,
        )

    def key_wait(s):
        slot = k_all.at[(j + 4 - s) % 4]
        pltpu.make_async_remote_copy(
            src_ref=slot,
            dst_ref=slot,
            send_sem=key_send.at[s],
            recv_sem=key_recv.at[s],
            device_id=at((j + s) % 4, g),
            device_id_type=MESH,
        ).wait_recv()

    group_wait(0)
    for s in range(1, 4):
        key_copy(s).start()

    group_wait(1)
    denom[...] = jnp.zeros_like(denom)

    def scores(chunk):
        later = jnp.where(chunk > j, TOK, jnp.where(chunk < j, -TOK, 0))
        for i in range(4):
            first = i * TOK
            key_block = k_all[chunk, first : first + TOK, :]
            for h in range(GROUP_HEADS):
                raw = lax.dot_general(
                    key_block,
                    q_g[first:PART, h * HEAD_DIM : (h + 1) * HEAD_DIM],
                    (((1,), (1,)), ((), ())),
                    preferred_element_type=jnp.float32,
                )
                e = jnp.exp(soft_cap * jnp.tanh(raw * (HEAD_DIM**-0.5 / soft_cap)))
                u = lax.broadcasted_iota(jnp.int32, raw.shape, 0)
                t = lax.broadcasted_iota(jnp.int32, raw.shape, 1)
                e = jnp.where((u + later <= t) | (t >= TOK), e, 0.0)
                cols = slice(h * PART + first, (h + 1) * PART)
                expo[chunk, first : first + TOK, cols] = e.astype(jnp.bfloat16)
                denom[:, cols] += jnp.sum(e, axis=0, keepdims=True)

    scores(j)
    swap(0)

    @pl.loop(1, 4)
    def _(s):
        key_wait(s)
        scores((j + 4 - s) % 4)

    swap(1)
    swap(2)

    group_wait(2)
    for h in range(GROUP_HEADS):
        cols = slice(h * PART, (h + 1) * PART)
        inverse = jnp.transpose(jnp.broadcast_to(1.0 / denom[:, cols], (128, PART)))
        heads = c_g[:, h * HEAD_DIM : (h + 1) * HEAD_DIM].astype(jnp.float32)
        for half in range(2):
            lanes = slice(half * 128, (half + 1) * 128)
            cots[cols, lanes] = (heads[:, lanes] * inverse).astype(jnp.bfloat16)

    def dv_copy(s):
        return pltpu.make_async_remote_copy(
            src_ref=dv_out.at[s],
            dst_ref=dv_in.at[s],
            send_sem=dv_send.at[s],
            recv_sem=dv_recv.at[s],
            device_id=at((j + 4 - s) % 4, g),
            device_id_type=MESH,
        )

    def dv_rows(chunk, i):
        first = i * TOK
        total = None
        for h in range(GROUP_HEADS):
            cols = slice(h * PART + first, (h + 1) * PART)
            term = jnp.dot(
                expo[chunk, first : first + TOK, cols],
                cots[cols, :],
                preferred_element_type=jnp.float32,
            )
            total = term if total is None else total + term
        return total

    @pl.loop(1, 4)
    def _(s):
        for i in range(4):
            dv_out[s, i * TOK : (i + 1) * TOK] = dv_rows((j + 4 - s) % 4, i).astype(jnp.bfloat16)
        dv_copy(s).start()

    for i in range(4):
        dv_acc[i * TOK : (i + 1) * TOK] = dv_rows(j, i)

    x_wait(0)
    x_copy(4).start()
    x_wait(2)
    x_copy(5).start()

    serve(0)

    local_copy(3).wait()

    def turn(half):
        for route in ((1, 4), (3, 5))[half]:
            x_wait(route)

        @pl.loop(0, X_HALF // 128)
        def _(i):
            first = pl.multiple_of(half * X_HALF + i * 128, 128)
            x_t[pl.ds(first, 128), :] = jnp.transpose(x_g[:, pl.ds(first, 128)])

    turn(0)

    for s in range(1, 4):
        dv_copy(s).wait_recv()
        dv_acc[...] += dv_in[s].astype(jnp.float32)

    def gr_copy(s, half):
        rows = pl.ds(half * 2 * ROWS, 2 * ROWS)
        return pltpu.make_async_remote_copy(
            src_ref=gr_out.at[s, rows],
            dst_ref=gr_in.at[s, rows],
            send_sem=gr_send.at[half, s],
            recv_sem=gr_recv.at[half, s],
            device_id=at((j + s) % 4, g),
            device_id_type=MESH,
        )

    dv_low = dv_acc[...].astype(jnp.bfloat16)

    def rows_of(quarter, i):
        first = pl.multiple_of((i * QUARTERS + quarter) * ROWS, 16)
        return jnp.dot(x_t[pl.ds(first, ROWS), :], dv_low, preferred_element_type=jnp.float32)

    def spread(half):
        blocks = (2 * half, 2 * half + 1)
        for s in range(1, 4):
            for i in blocks:
                gr_out[s, i * ROWS : (i + 1) * ROWS] = rows_of((j + s) % 4, i).astype(jnp.bfloat16)
            gr_copy(s, half).start()
        for i in blocks:
            gr_acc[i * ROWS : (i + 1) * ROWS] = rows_of(j, i)

    def own_copy(i):
        return pltpu.make_async_remote_copy(
            src_ref=sum_out.at[pl.ds(i * ROWS, ROWS)],
            dst_ref=grad.at[g],
            send_sem=own_send.at[i],
            recv_sem=own_recv.at[g],
            device_id=at(j, i),
            device_id_type=MESH,
        )

    def deliver(half):
        rows = slice(half * 2 * ROWS, (half + 1) * 2 * ROWS)
        total = gr_acc[rows]
        for s in range(1, 4):
            gr_copy(s, half).wait_recv()
            total += gr_in[s, rows].astype(jnp.float32)
        sum_out[rows] = total.astype(jnp.bfloat16)
        for i in (2 * half, 2 * half + 1):
            pl.when(g != i)(lambda: own_copy(i).start())

            @pl.when(g == i)
            def _(i=i):
                grad[i] = sum_out[i * ROWS : (i + 1) * ROWS]

    spread(0)
    serve(1)
    serve(2)
    turn(1)
    spread(1)
    deliver(0)
    deliver(1)

    for s in range(1, 4):
        peer = (g + s) % 4
        slot = grad.at[peer]
        pltpu.make_async_remote_copy(
            src_ref=slot,
            dst_ref=slot,
            send_sem=own_send.at[peer],
            recv_sem=own_recv.at[peer],
            device_id=at(j, peer),
            device_id_type=MESH,
        ).wait_recv()

    grad_copy = pltpu.make_async_copy(grad, grad_out, out_sem.at[0])
    grad_copy.start()

    for part in range(3):
        in_all(
            part,
            lambda n: bulk(part, n, deal_send.at[part], pick_recv.at[part]).wait_send(),
        )
        for role in range(2):
            has(part, cuts[role], lambda: swap_copy(part, role).wait_send())
    for part in range(3):
        in_all(
            part,
            lambda n: bulk(part, n, deal_send.at[part], pick_recv.at[part]).wait_recv(),
        )

    source_copy = pltpu.make_async_copy(source, source_out, out_sem.at[1])
    source_copy.start()

    for s in range(1, 4):
        for kind in range(3):
            group_copy(kind, s).wait_send()

        key_copy(s).wait_send()
        dv_copy(s).wait_send()
        gr_copy(s, 0).wait_send()
        gr_copy(s, 1).wait_send()
        own_copy((g + s) % 4).wait_send()
    for route in range(6):
        x_copy(route).wait_send()

    for part in range(3):
        for role in range(2):
            has(
                part,
                cuts[role],
                lambda: bulk(part, 15, pick_send.at[part], pick_recv.at[part]).wait_send(),
            )

    grad_copy.wait()
    source_copy.wait()


def plain_exchange(
    winners, w_in, m_in, v_in, source_out,
    w_own, m_own, v_own, state, dealt_0, dealt_1, dealt_2, picked_0, picked_1, picked_2, source,
    own_sem, out_sem, deal_send, deal_recv, pick_send, pick_recv,
):
    me = lax.axis_index("member")
    mine = lax.axis_index("fsdp")

    state_copies = [
        pltpu.make_async_copy(src, dst, own_sem.at[i])
        for i, (src, dst) in enumerate(((w_in, w_own), (m_in, m_own), (v_in, v_own)))
    ]
    for copy in state_copies:
        copy.start()

    barrier = pltpu.get_barrier_semaphore()

    @pl.loop(1, MEMBERS)
    def _(s):
        pl.semaphore_signal(
            barrier, inc=1, device_id={"member": (me + s) % MEMBERS}, device_id_type=MESH
        )

    for copy in state_copies:
        copy.wait()
    for band in range(8):
        cols = slice(band * 128, (band + 1) * 128)
        state[band, 0:ROWS] = w_own[:, cols]
        state[band, ROWS : 2 * ROWS] = m_own[:, cols].astype(jnp.bfloat16)
        state[band, 2 * ROWS : 3 * ROWS] = v_own[:, cols].astype(jnp.bfloat16)
    pl.semaphore_wait(barrier, MEMBERS - 1)

    core = mine % 2
    starts, sizes = (0, 48, 80), (48, 32, 16)
    dealt, picked = (dealt_0, dealt_1, dealt_2), (picked_0, picked_1, picked_2)

    def extra(member):
        return (member + 2 * core) % 4 == 1

    def sorts(member, part, action):
        if part < 2:
            action()
        else:
            pl.when(extra(member))(action)

    def place(ref, member, part):
        first = member % 4 * PIECE + starts[part] if part < 2 else 4 * PIECE
        return ref.at[member // 4, pl.ds(first, sizes[part])]

    def deal_copy(s, part):
        peer = (me + s) % MEMBERS
        return pltpu.make_async_remote_copy(
            src_ref=place(state, peer, part),
            dst_ref=dealt[part].at[me],
            send_sem=deal_send.at[part],
            recv_sem=deal_recv.at[part],
            device_id={"member": peer},
            device_id_type=MESH,
        )

    def all_of(part, count, send_sem, recv_sem):
        ref = dealt[part].at[pl.ds(0, count)]
        return pltpu.make_async_remote_copy(
            src_ref=ref,
            dst_ref=ref,
            send_sem=send_sem.at[part],
            recv_sem=recv_sem.at[part],
            device_id={"member": (me + 1) % MEMBERS},
            device_id_type=MESH,
        )

    def to_or_from_sorters(part, wait):
        if part < 2:
            wait(MEMBERS - 1)
        else:
            pl.when(extra(me))(lambda: wait(MEMBERS // 4 - 1))
            pl.when(jnp.logical_not(extra(me)))(lambda: wait(MEMBERS // 4))

    for part in range(3):

        @pl.loop(1, MEMBERS)
        def _(s):
            sorts((me + s) % MEMBERS, part, lambda: deal_copy(s, part).start())

    def keep(part):
        dealt[part][me] = place(state, me, part)[...]

    for part in range(3):
        sorts(me, part, lambda: keep(part))

    def pick_copy(s, part):
        peer = (me + s) % MEMBERS
        return pltpu.make_async_remote_copy(
            src_ref=picked[part].at[s],
            dst_ref=place(source, me, part),
            send_sem=pick_send.at[part],
            recv_sem=pick_recv.at[part],
            device_id={"member": peer},
            device_id_type=MESH,
        )

    def pick(part):
        def action():
            all_of(part, MEMBERS - 1, deal_send, deal_recv).wait_recv()

            @pl.loop(1, MEMBERS)
            def _(s):
                picked[part][s] = dealt[part][winners[(me + s) % MEMBERS]]
                pick_copy(s, part).start()

            place(source, me, part)[...] = dealt[part][winners[me]]

        sorts(me, part, action)

    for part in range(3):
        pick(part)
    for part in range(3):
        to_or_from_sorters(
            part, lambda count: all_of(part, count, deal_send, deal_recv).wait_send()
        )
    for part in range(3):
        to_or_from_sorters(
            part, lambda count: all_of(part, count, pick_send, pick_recv).wait_recv()
        )

    source_copy = pltpu.make_async_copy(source, source_out, out_sem.at[0])
    source_copy.start()
    for part in range(3):
        sorts(
            me, part, lambda: all_of(part, MEMBERS - 1, pick_send, pick_recv).wait_send()
        )
    source_copy.wait()


def adam_kernel(grad, source, new_w, new_m, new_v):
    for band in range(8):
        cols = slice(band * 128, (band + 1) * 128)
        lanes = slice(band % 2 * 128, band % 2 * 128 + 128)
        gradient = grad[band // 2, :, lanes].astype(jnp.float32)
        old_w = source[band, 0:ROWS].astype(jnp.float32)
        old_m = source[band, ROWS : 2 * ROWS].astype(jnp.float32)
        old_v = source[band, 2 * ROWS : 3 * ROWS].astype(jnp.float32)
        first = beta_one * old_m + (1.0 - beta_one) * gradient
        second = beta_two * old_v + (1.0 - beta_two) * gradient * gradient
        first_hat = first * (1.0 / (1.0 - beta_one**adam_step))
        second_hat = second * (1.0 / (1.0 - beta_two**adam_step))
        update = first_hat / (jnp.sqrt(second_hat) + adam_eps) + decay_rate * old_w
        new_w[:, cols] = (old_w - learning_rate * update).astype(jnp.bfloat16)
        new_m[:, cols] = first
        new_v[:, cols] = second


def local(inputs, queries, keys, cotangent, winners, weights, first_moment, second_moment):
    f32, bf16 = jnp.float32, jnp.bfloat16
    vmem = pl.BlockSpec(memory_space=pltpu.VMEM)
    hbm = pl.BlockSpec(memory_space=pltpu.HBM)
    dma = pltpu.SemaphoreType.DMA
    scratch = [
        pltpu.VMEM((QUARTERS, PART, HEAD_DIM), bf16),
        pltpu.VMEM((PART, GROUP_HEADS * HEAD_DIM), bf16),
        pltpu.VMEM((PART, GROUP_HEADS * HEAD_DIM), bf16),
        pltpu.VMEM((PART, FEAT), bf16),
        pltpu.VMEM((FEAT, PART), bf16),
        pltpu.VMEM((QUARTERS, PART, GROUP_HEADS * PART), bf16),
        pltpu.VMEM((1, GROUP_HEADS * PART), f32),
        pltpu.VMEM((GROUP_HEADS * PART, HEAD_DIM), bf16),
        pltpu.VMEM((PART, HEAD_DIM), f32),
        pltpu.VMEM((4, PART, HEAD_DIM), bf16),
        pltpu.VMEM((4, PART, HEAD_DIM), bf16),
        pltpu.VMEM((4 * ROWS, HEAD_DIM), f32),
        pltpu.VMEM((4, 4 * ROWS, HEAD_DIM), bf16),
        pltpu.VMEM((4, 4 * ROWS, HEAD_DIM), bf16),
        pltpu.VMEM((4 * ROWS, HEAD_DIM), bf16),
        pltpu.VMEM((4, ROWS, HEAD_DIM), bf16),
    ]
    own_state = [
        pltpu.VMEM((ROWS, KVW), bf16),
        pltpu.VMEM((ROWS, KVW), f32),
        pltpu.VMEM((ROWS, KVW), f32),
        pltpu.VMEM((8, 3 * ROWS, 128), bf16),
    ]
    landing = pltpu.VMEM((8, 3 * ROWS, 128), bf16)
    parts = []
    for rows in (48, 32, 16):
        for count in (16, SLOTS, SLOTS, 16):
            parts += [pltpu.VMEM((count, rows, 128), bf16)] * 2
    parts += [pltpu.VMEM((30, rows, 128), bf16) for rows in (48, 32, 16)]
    state_args = (weights[0], first_moment[0], second_moment[0])
    state_shape = jax.ShapeDtypeStruct((8, 3 * ROWS, 128), bf16)
    smem = pl.BlockSpec(memory_space=pltpu.SMEM)
    grad, source, flag = pl.pallas_call(
        kernel,
        out_shape=(
            jax.ShapeDtypeStruct((4, ROWS, HEAD_DIM), bf16),
            state_shape,
            jax.ShapeDtypeStruct((1,), jnp.int32),
        ),
        in_specs=[smem] + [hbm] * 7,
        out_specs=(hbm, hbm, smem),
        scratch_shapes=scratch
        + own_state
        + [landing, pltpu.VMEM((8, 128), jnp.int32), pltpu.SMEM((8, 128), jnp.int32)]
        + [dma((4,)), dma((3,)), dma((3,)), dma((4, 4)), dma((4, 4))]
        + [dma((4,))] * 4
        + [dma((2, 4)), dma((2, 4)), dma((4,)), dma((4,)), dma((6,)), dma((6,))]
        + [dma((3,)), dma((3, 2)), dma((3, 2)), dma((3, 2)), dma((3,)), dma((3,))]
        + parts,
        compiler_params=pltpu.CompilerParams(
            collective_id=0, has_side_effects=True, vmem_limit_bytes=VMEM_LIMIT
        ),
        cost_estimate=pl.CostEstimate(
            flops=3_000_000_000, bytes_accessed=6_000_000, transcendentals=4_000_000
        ),
    )(winners, inputs[0], queries[0], keys[0], cotangent[0], *state_args)

    def step(grad, source):
        return pl.pallas_call(
            adam_kernel,
            out_shape=(
                jax.ShapeDtypeStruct((ROWS, KVW), bf16),
                jax.ShapeDtypeStruct((ROWS, KVW), f32),
                jax.ShapeDtypeStruct((ROWS, KVW), f32),
            ),
            in_specs=[vmem, vmem],
            out_specs=(vmem, vmem, vmem),
            compiler_params=pltpu.CompilerParams(vmem_limit_bytes=VMEM_LIMIT),
        )(grad, source)

    def crowded():
        all_source = pl.pallas_call(
            plain_exchange,
            out_shape=state_shape,
            in_specs=[smem] + [hbm] * 3,
            out_specs=hbm,
            scratch_shapes=own_state
            + [pltpu.VMEM((MEMBERS, rows, 128), bf16) for rows in (48, 32, 16)] * 2
            + [landing, dma((3,)), dma((1,))]
            + [dma((3,))] * 4,
            compiler_params=pltpu.CompilerParams(
                collective_id=1, has_side_effects=True, vmem_limit_bytes=VMEM_LIMIT
            ),
        )(winners, *state_args)
        return step(grad, all_source)

    outs = lax.cond(flag[0] > 0, crowded, lambda: step(grad, source))
    return tuple(out[None] for out in outs)


def solution(mesh):
    rows = P("member", "fsdp", None)
    return jax.shard_map(
        local,
        mesh=mesh,
        in_specs=(rows, rows, rows, rows, P(), rows, rows, rows),
        out_specs=(rows, rows, rows),
        check_vma=False,
    )
```

```python
import jax
import jax.numpy as jnp
from jax import lax
from jax.experimental import pallas as pl
from jax.experimental.pallas import tpu as pltpu
from jax.sharding import PartitionSpec as P

MEMBERS = 32
KV_HEADS = 4
QUARTERS = 4
HEAD_DIM = 256
GROUP_HEADS = 2
TOK = 128
FEAT = 1792
X_HALF = 896
ROWS = 112
KVW = 1024
PART = QUARTERS * TOK
PIECE = 80
RING = 16
HALF = 8
SLOTS = 5
BLOCKS = 7

beta_one = 0.9
beta_two = 0.999
learning_rate = 0.001
decay_rate = 0.1
adam_eps = 1e-08
adam_step = 200
soft_cap = 50.0

VMEM_LIMIT = 60 * 1024 * 1024

MESH = pl.DeviceIdType.MESH


def kernel(
    winners, x_in, q_in, k_in, c_in, w_in, m_in, v_in,
    grad_out, source_out, flag_out,
    k_all, q_g, c_g, x_g, x_t, expo, denom, cots,
    dv_acc, dv_out, dv_in, gr_acc, gr_out, gr_in, sum_out, grad,
    w_own, m_own, v_own, state, source, table_v, table_s,
    loc_sem, own_sem, out_sem, grp_send, grp_recv, key_send, key_recv, dv_send, dv_recv,
    gr_send, gr_recv, own_send, own_recv, x_send, x_recv, deal_send, deal_recv, swap_send, swap_recv,
    pick_send, pick_recv, *parts,
):
    me = lax.axis_index("member")
    mine = lax.axis_index("fsdp")
    dealt, swap_out, swap_in, sent = (
        [(parts[8 * part + 2 * kind], parts[8 * part + 2 * kind + 1]) for part in range(3)]
        for kind in range(4)
    )
    both = parts[24:27]
    g = mine // QUARTERS
    j = mine % QUARTERS

    sibling = j + 1 - 2 * (j % 2)
    across = (j + 2) % QUARTERS
    diagonal = (sibling + 2) % QUARTERS

    def at(quarter, head):
        return {"fsdp": head * QUARTERS + quarter}

    state_copies = [
        pltpu.make_async_copy(src, dst, own_sem.at[i])
        for i, (src, dst) in enumerate(((w_in, w_own), (m_in, m_own), (v_in, v_own)))
    ]
    for copy in state_copies:
        copy.start()

    barrier = pltpu.get_barrier_semaphore()
    for s in range(1, 4):
        pl.semaphore_signal(
            barrier, inc=1, device_id=at(j, (g + s) % 4), device_id_type=MESH
        )
        pl.semaphore_signal(
            barrier, inc=1, device_id=at((j + s) % 4, g), device_id_type=MESH
        )

    def greet(offset, row):
        pl.semaphore_signal(
            barrier,
            inc=1,
            device_id={
                "member": (me // RING + row) % 2 * RING + (me + RING + offset) % RING
            },
            device_id_type=MESH,
        )

    @pl.loop(1, 6)
    def _(s):
        for row in range(2):
            greet(s, row)
            greet(-s, row)

    greet(0, 1)

    def own_slot(kind, owner):
        rows = pl.ds(owner * TOK, TOK)
        return (k_all.at[j, rows], q_g.at[rows], c_g.at[rows], x_g.at[rows])[kind]

    def own_slice(kind, head):
        if kind == 0:
            return k_in.at[:, pl.ds(head * HEAD_DIM, HEAD_DIM)]
        if kind == 3:
            return x_in
        wide = GROUP_HEADS * HEAD_DIM
        return (q_in, c_in)[kind - 1].at[:, pl.ds(head * wide, wide)]

    def group_copy(kind, s):
        peer = (g + s) % 4
        return pltpu.make_async_remote_copy(
            src_ref=own_slice(kind, peer),
            dst_ref=own_slot(kind, g),
            send_sem=grp_send.at[kind, s],
            recv_sem=grp_recv.at[kind, s],
            device_id=at(j, peer),
            device_id_type=MESH,
        )

    def group_wait(kind):
        for s in range(1, 4):
            slot = own_slot(kind, (g + 4 - s) % 4)
            pltpu.make_async_remote_copy(
                src_ref=slot,
                dst_ref=slot,
                send_sem=grp_send.at[kind, s],
                recv_sem=grp_recv.at[kind, s],
                device_id=at(j, (g + s) % 4),
                device_id_type=MESH,
            ).wait_recv()
        local_copy(kind).wait()

    def local_copy(kind):
        return pltpu.make_async_copy(own_slice(kind, g), own_slot(kind, g), loc_sem.at[kind])

    for kind in range(4):
        local_copy(kind).start()

    pl.semaphore_wait(barrier, 6 + 21)

    for kind in range(3):
        for s in range(1, 4):
            group_copy(kind, s).start()

    for copy in state_copies:
        copy.wait()
    for band in range(8):
        cols = slice(band * 128, (band + 1) * 128)
        state[band, 0:ROWS] = w_own[:, cols]
        state[band, ROWS : 2 * ROWS] = m_own[:, cols].astype(jnp.bfloat16)
        state[band, 2 * ROWS : 3 * ROWS] = v_own[:, cols].astype(jnp.bfloat16)

    core = mine % 2
    y = me // RING
    z = me % RING
    starts, sizes = (0, 48, 80), (48, 32, 16)
    cuts = ((z + RING - 5) % RING, (z + RING - 10) % RING)
    reach = (5, 2)

    def special(r):
        return (r + 2 * core) % 4 == 1

    def has(part, r, action):
        if part < 2:
            action()
        else:
            pl.when(special(r))(action)

    def place(ref, r, part, row=None):
        piece = (y if row is None else row) * RING + r
        first = piece % 4 * PIECE + starts[part] if part < 2 else 4 * PIECE
        return ref.at[piece // 4, pl.ds(first, sizes[part])]

    def bulk(part, count, send_sem, recv_sem):
        ref = sent[part][0].at[pl.ds(0, 15)] if count == 15 else both[part].at[pl.ds(0, count)]
        return pltpu.make_async_remote_copy(
            src_ref=ref,
            dst_ref=ref,
            send_sem=send_sem,
            recv_sem=recv_sem,
            device_id={"member": (me + 1) % MEMBERS},
            device_id_type=MESH,
        )

    def in_all(part, wait):
        if part < 2:
            wait(30)
        else:
            either = special(cuts[0]) | special(cuts[1])
            pl.when(either)(lambda: wait(7))
            pl.when(jnp.logical_not(either))(lambda: wait(8))

    def deal(part):
        @pl.loop(0, HALF)
        def _(d):
            for role in range(2):
                r = (z + RING - HALF * role - d) % RING
                for row in range(2):

                    def start(role=role, row=row, r=r):
                        pltpu.make_async_remote_copy(
                            src_ref=place(state, r, part, row),
                            dst_ref=dealt[part][role].at[y * HALF + d],
                            send_sem=deal_send.at[part],
                            recv_sem=deal_recv.at[part, role],
                            device_id={
                                "member": row * RING + (z + RING + reach[role] - d) % RING
                            },
                            device_id_type=MESH,
                        ).start()

                    other = (d != reach[role]) | (y != row)
                    pl.when(other if part < 2 else other & special(r))(start)

        for role in range(2):

            def keep(role=role):
                dealt[part][role][y * HALF + reach[role]] = place(state, cuts[role], part)[...]

            has(part, cuts[role], keep)

    def seat(member, role):
        return member // RING * HALF + (member % RING + RING - cuts[role]) % HALF

    def swap_copy(part, role):
        partner = (z + 5) % RING if role == 0 else (z + RING - 5) % RING
        return pltpu.make_async_remote_copy(
            src_ref=swap_out[part][role],
            dst_ref=swap_in[part][1 - role],
            send_sem=swap_send.at[part, role],
            recv_sem=swap_recv.at[part, 1 - role],
            device_id={"member": y * RING + partner},
            device_id_type=MESH,
        )

    def swap(part):
        for role in range(2):

            def action(role=role):
                bulk(part, 15, deal_send.at[part], deal_recv.at[part, role]).wait_recv()
                for k in range(SLOTS):
                    swap_out[part][role][k] = dealt[part][role][seat(table_s[2 * role, k], role)]
                swap_copy(part, role).start()

            has(part, cuts[role], action)

    def serve(part):
        for role in range(2):

            def action(role=role):
                swap_copy(part, 1 - role).wait_recv()

                @pl.loop(0, HALF)
                def _(d):
                    for row in range(2):
                        member = row * RING + (z + RING - reach[role] + d) % RING
                        winner = winners[member]
                        inside = (winner % RING + RING - cuts[role]) % RING // HALF == role
                        near = dealt[part][role][seat(winner, role)]
                        rank = jnp.minimum(table_s[2 * role + 1, winner], SLOTS - 1)
                        far = swap_in[part][role][rank]
                        sent[part][role][row * HALF + d] = jnp.where(inside, near, far)

                        def start(row=row, member=member):
                            pltpu.make_async_remote_copy(
                                src_ref=sent[part][role].at[row * HALF + d],
                                dst_ref=place(source, cuts[role], part),
                                send_sem=pick_send.at[part],
                                recv_sem=pick_recv.at[part],
                                device_id={"member": member},
                                device_id_type=MESH,
                            ).start()

                        pl.when((d != reach[role]) | (y != row))(start)

                place(source, cuts[role], part)[...] = sent[part][role][y * HALF + reach[role]]

            has(part, cuts[role], action)

    for part in range(3):
        deal(part)

    right, left = (g + 1) % 4, (g + 3) % 4
    routes = ((0, g, right), (0, g, left), (1, g, left), (1, g, right), (0, left, right), (1, right, left))
    x_from = (left, right, right, left, left, right)
    x_owner = (left, right, right, left, (g + 2) % 4, (g + 2) % 4)

    def x_slot(owner, half):
        return x_g.at[pl.ds(owner * TOK, TOK), pl.ds(half * X_HALF, X_HALF)]

    def x_copy(route):
        half, owner, peer = routes[route]
        slot = x_slot(owner, half)
        return pltpu.make_async_remote_copy(
            src_ref=slot if route > 3 else x_in.at[:, pl.ds(half * X_HALF, X_HALF)],
            dst_ref=slot,
            send_sem=x_send.at[route],
            recv_sem=x_recv.at[route],
            device_id=at(j, peer),
            device_id_type=MESH,
        )

    def x_wait(route):
        slot = x_slot(x_owner[route], routes[route][0])
        pltpu.make_async_remote_copy(
            src_ref=slot,
            dst_ref=slot,
            send_sem=x_send.at[route],
            recv_sem=x_recv.at[route],
            device_id=at(j, x_from[route]),
            device_id_type=MESH,
        ).wait_recv()

    for route in range(4):
        x_copy(route).start()

    shape = (MEMBERS, 128)
    sub = lax.broadcasted_iota(jnp.int32, shape, 0)
    lane = lax.broadcasted_iota(jnp.int32, shape, 1)
    by_sub = jnp.zeros(shape, jnp.int32)
    by_lane = jnp.full(shape, -1, jnp.int32)
    for b in range(MEMBERS):
        by_sub = jnp.where(sub == b, winners[b], by_sub)
        by_lane = jnp.where(lane == b, winners[b], by_lane)
    one, none = jnp.ones(shape, jnp.int32), jnp.zeros(shape, jnp.int32)
    takes = jnp.where(by_lane == sub, one, none)
    taken = jnp.where(by_sub == lane, one, none)

    def inside_of(index, r, role):
        return jnp.where((index % RING + RING - r) % RING // HALF == role, one, none)

    def needed_by(r, role):
        in_sub, in_lane = inside_of(sub, r, role), inside_of(lane, r, role)
        out_sub = in_sub * jnp.max(takes * (1 - in_lane), axis=1, keepdims=True)
        return in_sub, in_lane, out_sub

    for role in range(2):
        in_sub, in_lane, out_sub = needed_by(cuts[role], role)
        out_lane = in_lane * jnp.max(taken * (1 - in_sub), axis=0, keepdims=True)
        rank = jnp.sum(jnp.where(lane < sub, out_lane, none), axis=1, keepdims=True)
        chosen = jnp.where(rank == lane, out_sub * sub, none)
        table_v[2 * role : 2 * role + 1, :] = jnp.sum(chosen, axis=0, keepdims=True)
        in_need = (1 - in_sub) * jnp.max(takes * in_lane, axis=1, keepdims=True)
        table_v[2 * role + 1 : 2 * role + 2, :] = jnp.sum(
            jnp.where(sub < lane, in_need, none), axis=0, keepdims=True
        )
    table_copy = pltpu.make_async_copy(table_v, table_s, out_sem.at[2])
    table_copy.start()

    most = jnp.zeros((1, 128), jnp.int32)
    for r in range(RING):
        most = jnp.maximum(most, jnp.sum(needed_by(r, 0)[2], axis=0, keepdims=True))
    flag_out[0] = jnp.max(jnp.where(most > SLOTS, 1, 0))
    table_copy.wait()

    def key_copy(route):
        slot = k_all.at[across if route == 2 else j]
        return pltpu.make_async_remote_copy(
            src_ref=slot,
            dst_ref=slot,
            send_sem=key_send.at[route],
            recv_sem=key_recv.at[route],
            device_id=at(across if route == 1 else sibling, g),
            device_id_type=MESH,
        )

    def key_wait(route):
        slot = k_all.at[(sibling, across, diagonal)[route]]
        pltpu.make_async_remote_copy(
            src_ref=slot,
            dst_ref=slot,
            send_sem=key_send.at[route],
            recv_sem=key_recv.at[route],
            device_id=at(across if route == 1 else sibling, g),
            device_id_type=MESH,
        ).wait_recv()

    group_wait(0)
    key_copy(1).start()
    key_copy(0).start()

    group_wait(1)
    denom[...] = jnp.zeros_like(denom)

    def scores(chunk):
        later = jnp.where(chunk > j, TOK, jnp.where(chunk < j, -TOK, 0))
        for i in range(4):
            first = i * TOK
            key_block = k_all[chunk, first : first + TOK, :]
            for h in range(GROUP_HEADS):
                raw = lax.dot_general(
                    key_block,
                    q_g[first:PART, h * HEAD_DIM : (h + 1) * HEAD_DIM],
                    (((1,), (1,)), ((), ())),
                    preferred_element_type=jnp.float32,
                )
                e = jnp.exp(soft_cap * jnp.tanh(raw * (HEAD_DIM**-0.5 / soft_cap)))
                u = lax.broadcasted_iota(jnp.int32, raw.shape, 0)
                t = lax.broadcasted_iota(jnp.int32, raw.shape, 1)
                e = jnp.where((u + later <= t) | (t >= TOK), e, 0.0)
                cols = slice(h * PART + first, (h + 1) * PART)
                expo[chunk, first : first + TOK, cols] = e.astype(jnp.bfloat16)
                denom[:, cols] += jnp.sum(e, axis=0, keepdims=True)

    scores(j)
    swap(0)

    key_wait(1)
    key_copy(2).start()
    key_wait(0)

    @pl.loop(0, 3)
    def _(s):
        pl.when(s == 2)(lambda: key_wait(2))
        scores(jnp.where(s == 0, sibling, jnp.where(s == 1, across, diagonal)))

    swap(1)
    swap(2)

    group_wait(2)
    for h in range(GROUP_HEADS):
        cols = slice(h * PART, (h + 1) * PART)
        inverse = jnp.transpose(jnp.broadcast_to(1.0 / denom[:, cols], (128, PART)))
        heads = c_g[:, h * HEAD_DIM : (h + 1) * HEAD_DIM].astype(jnp.float32)
        for half in range(2):
            lanes = slice(half * 128, (half + 1) * 128)
            cots[cols, lanes] = (heads[:, lanes] * inverse).astype(jnp.bfloat16)

    def dv_copy(slot):
        return pltpu.make_async_remote_copy(
            src_ref=dv_out.at[slot],
            dst_ref=dv_in.at[slot],
            send_sem=dv_send.at[slot],
            recv_sem=dv_recv.at[slot],
            device_id=at(across if slot == 2 else sibling, g),
            device_id_type=MESH,
        )

    def dv_rows(chunk, i):
        first = i * TOK
        total = None
        for h in range(GROUP_HEADS):
            cols = slice(h * PART + first, (h + 1) * PART)
            term = jnp.dot(
                expo[chunk, first : first + TOK, cols],
                cots[cols, :],
                preferred_element_type=jnp.float32,
            )
            total = term if total is None else total + term
        return total

    for slot, chunk in ((1, diagonal), (0, sibling)):
        for i in range(4):
            dv_out[slot, i * TOK : (i + 1) * TOK] = dv_rows(chunk, i).astype(jnp.bfloat16)
        dv_copy(slot).start()

    @pl.loop(0, 2)
    def _(step):
        chunk = jnp.where(step == 0, across, j)
        for i in range(4):
            dv_acc[step, i * TOK : (i + 1) * TOK] = dv_rows(chunk, i)

    dv_copy(1).wait_recv()
    dv_out[2] = (dv_acc[0] + dv_in[1].astype(jnp.float32)).astype(jnp.bfloat16)
    dv_copy(2).start()

    serve(0)

    x_wait(0)
    x_copy(4).start()
    x_wait(2)
    x_copy(5).start()

    serve(1)
    serve(2)

    local_copy(3).wait()

    def turn(half):
        for route in ((1, 4), (3, 5))[half]:
            x_wait(route)

        @pl.loop(0, X_HALF // 128)
        def _(i):
            first = pl.multiple_of(half * X_HALF + i * 128, 128)
            x_t[pl.ds(first, 128), :] = jnp.transpose(x_g[:, pl.ds(first, 128)])

    turn(0)

    dv_copy(0).wait_recv()
    dv_copy(2).wait_recv()
    dv_low = (
        dv_acc[1] + dv_in[0].astype(jnp.float32) + dv_in[2].astype(jnp.float32)
    ).astype(jnp.bfloat16)

    def gr_copy(slot, half):
        rows = pl.ds(half * 2 * ROWS, 2 * ROWS)
        return pltpu.make_async_remote_copy(
            src_ref=gr_out.at[slot, rows],
            dst_ref=gr_in.at[slot, rows],
            send_sem=gr_send.at[half, slot],
            recv_sem=gr_recv.at[half, slot],
            device_id=at(across if slot == 2 else sibling, g),
            device_id_type=MESH,
        )

    def rows_of(quarter, i):
        first = pl.multiple_of((i * QUARTERS + quarter) * ROWS, 16)
        return jnp.dot(x_t[pl.ds(first, ROWS), :], dv_low, preferred_element_type=jnp.float32)

    def spread(half):
        blocks = (2 * half, 2 * half + 1)
        rows = slice(half * 2 * ROWS, (half + 1) * 2 * ROWS)
        for slot, quarter in ((1, diagonal), (0, sibling)):
            for i in blocks:
                gr_out[slot, i * ROWS : (i + 1) * ROWS] = rows_of(quarter, i).astype(jnp.bfloat16)
            gr_copy(slot, half).start()
        for slot, quarter in ((0, across), (1, j)):
            for i in blocks:
                gr_acc[slot, i * ROWS : (i + 1) * ROWS] = rows_of(quarter, i)
        gr_copy(1, half).wait_recv()
        gr_out[2, rows] = (gr_acc[0, rows] + gr_in[1, rows].astype(jnp.float32)).astype(
            jnp.bfloat16
        )
        gr_copy(2, half).start()

    def own_copy(i):
        return pltpu.make_async_remote_copy(
            src_ref=sum_out.at[pl.ds(i * ROWS, ROWS)],
            dst_ref=grad.at[g],
            send_sem=own_send.at[i],
            recv_sem=own_recv.at[g],
            device_id=at(j, i),
            device_id_type=MESH,
        )

    def deliver(half):
        rows = slice(half * 2 * ROWS, (half + 1) * 2 * ROWS)
        total = gr_acc[1, rows]
        for slot in (0, 2):
            gr_copy(slot, half).wait_recv()
            total += gr_in[slot, rows].astype(jnp.float32)
        sum_out[rows] = total.astype(jnp.bfloat16)
        for i in (2 * half, 2 * half + 1):
            pl.when(g != i)(lambda: own_copy(i).start())

            @pl.when(g == i)
            def _(i=i):
                grad[i] = sum_out[i * ROWS : (i + 1) * ROWS]

    spread(0)
    turn(1)
    spread(1)
    deliver(0)
    deliver(1)

    for s in range(1, 4):
        peer = (g + s) % 4
        slot = grad.at[peer]
        pltpu.make_async_remote_copy(
            src_ref=slot,
            dst_ref=slot,
            send_sem=own_send.at[peer],
            recv_sem=own_recv.at[peer],
            device_id=at(j, peer),
            device_id_type=MESH,
        ).wait_recv()

    grad_copy = pltpu.make_async_copy(grad, grad_out, out_sem.at[0])
    grad_copy.start()

    for part in range(3):
        in_all(
            part,
            lambda n: bulk(part, n, deal_send.at[part], pick_recv.at[part]).wait_send(),
        )
        for role in range(2):
            has(part, cuts[role], lambda: swap_copy(part, role).wait_send())
    for part in range(3):
        in_all(
            part,
            lambda n: bulk(part, n, deal_send.at[part], pick_recv.at[part]).wait_recv(),
        )

    source_copy = pltpu.make_async_copy(source, source_out, out_sem.at[1])
    source_copy.start()

    for s in range(1, 4):
        for kind in range(3):
            group_copy(kind, s).wait_send()

        key_copy(s - 1).wait_send()
        dv_copy(s - 1).wait_send()
        gr_copy(s - 1, 0).wait_send()
        gr_copy(s - 1, 1).wait_send()
        own_copy((g + s) % 4).wait_send()
    for route in range(6):
        x_copy(route).wait_send()

    for part in range(3):
        for role in range(2):
            has(
                part,
                cuts[role],
                lambda: bulk(part, 15, pick_send.at[part], pick_recv.at[part]).wait_send(),
            )

    grad_copy.wait()
    source_copy.wait()


def plain_exchange(
    winners, w_in, m_in, v_in, source_out,
    w_own, m_own, v_own, state, dealt_0, dealt_1, dealt_2, picked_0, picked_1, picked_2, source,
    own_sem, out_sem, deal_send, deal_recv, pick_send, pick_recv,
):
    me = lax.axis_index("member")
    mine = lax.axis_index("fsdp")

    state_copies = [
        pltpu.make_async_copy(src, dst, own_sem.at[i])
        for i, (src, dst) in enumerate(((w_in, w_own), (m_in, m_own), (v_in, v_own)))
    ]
    for copy in state_copies:
        copy.start()

    barrier = pltpu.get_barrier_semaphore()

    @pl.loop(1, MEMBERS)
    def _(s):
        pl.semaphore_signal(
            barrier, inc=1, device_id={"member": (me + s) % MEMBERS}, device_id_type=MESH
        )

    for copy in state_copies:
        copy.wait()
    for band in range(8):
        cols = slice(band * 128, (band + 1) * 128)
        state[band, 0:ROWS] = w_own[:, cols]
        state[band, ROWS : 2 * ROWS] = m_own[:, cols].astype(jnp.bfloat16)
        state[band, 2 * ROWS : 3 * ROWS] = v_own[:, cols].astype(jnp.bfloat16)
    pl.semaphore_wait(barrier, MEMBERS - 1)

    core = mine % 2
    starts, sizes = (0, 48, 80), (48, 32, 16)
    dealt, picked = (dealt_0, dealt_1, dealt_2), (picked_0, picked_1, picked_2)

    def extra(member):
        return (member + 2 * core) % 4 == 1

    def sorts(member, part, action):
        if part < 2:
            action()
        else:
            pl.when(extra(member))(action)

    def place(ref, member, part):
        first = member % 4 * PIECE + starts[part] if part < 2 else 4 * PIECE
        return ref.at[member // 4, pl.ds(first, sizes[part])]

    def deal_copy(s, part):
        peer = (me + s) % MEMBERS
        return pltpu.make_async_remote_copy(
            src_ref=place(state, peer, part),
            dst_ref=dealt[part].at[me],
            send_sem=deal_send.at[part],
            recv_sem=deal_recv.at[part],
            device_id={"member": peer},
            device_id_type=MESH,
        )

    def all_of(part, count, send_sem, recv_sem):
        ref = dealt[part].at[pl.ds(0, count)]
        return pltpu.make_async_remote_copy(
            src_ref=ref,
            dst_ref=ref,
            send_sem=send_sem.at[part],
            recv_sem=recv_sem.at[part],
            device_id={"member": (me + 1) % MEMBERS},
            device_id_type=MESH,
        )

    def to_or_from_sorters(part, wait):
        if part < 2:
            wait(MEMBERS - 1)
        else:
            pl.when(extra(me))(lambda: wait(MEMBERS // 4 - 1))
            pl.when(jnp.logical_not(extra(me)))(lambda: wait(MEMBERS // 4))

    for part in range(3):

        @pl.loop(1, MEMBERS)
        def _(s):
            sorts((me + s) % MEMBERS, part, lambda: deal_copy(s, part).start())

    def keep(part):
        dealt[part][me] = place(state, me, part)[...]

    for part in range(3):
        sorts(me, part, lambda: keep(part))

    def pick_copy(s, part):
        peer = (me + s) % MEMBERS
        return pltpu.make_async_remote_copy(
            src_ref=picked[part].at[s],
            dst_ref=place(source, me, part),
            send_sem=pick_send.at[part],
            recv_sem=pick_recv.at[part],
            device_id={"member": peer},
            device_id_type=MESH,
        )

    def pick(part):
        def action():
            all_of(part, MEMBERS - 1, deal_send, deal_recv).wait_recv()

            @pl.loop(1, MEMBERS)
            def _(s):
                picked[part][s] = dealt[part][winners[(me + s) % MEMBERS]]
                pick_copy(s, part).start()

            place(source, me, part)[...] = dealt[part][winners[me]]

        sorts(me, part, action)

    for part in range(3):
        pick(part)
    for part in range(3):
        to_or_from_sorters(
            part, lambda count: all_of(part, count, deal_send, deal_recv).wait_send()
        )
    for part in range(3):
        to_or_from_sorters(
            part, lambda count: all_of(part, count, pick_send, pick_recv).wait_recv()
        )

    source_copy = pltpu.make_async_copy(source, source_out, out_sem.at[0])
    source_copy.start()
    for part in range(3):
        sorts(
            me, part, lambda: all_of(part, MEMBERS - 1, pick_send, pick_recv).wait_send()
        )
    source_copy.wait()


def adam_kernel(grad, source, new_w, new_m, new_v):
    for band in range(8):
        cols = slice(band * 128, (band + 1) * 128)
        lanes = slice(band % 2 * 128, band % 2 * 128 + 128)
        gradient = grad[band // 2, :, lanes].astype(jnp.float32)
        old_w = source[band, 0:ROWS].astype(jnp.float32)
        old_m = source[band, ROWS : 2 * ROWS].astype(jnp.float32)
        old_v = source[band, 2 * ROWS : 3 * ROWS].astype(jnp.float32)
        first = beta_one * old_m + (1.0 - beta_one) * gradient
        second = beta_two * old_v + (1.0 - beta_two) * gradient * gradient
        first_hat = first * (1.0 / (1.0 - beta_one**adam_step))
        second_hat = second * (1.0 / (1.0 - beta_two**adam_step))
        update = first_hat / (jnp.sqrt(second_hat) + adam_eps) + decay_rate * old_w
        new_w[:, cols] = (old_w - learning_rate * update).astype(jnp.bfloat16)
        new_m[:, cols] = first
        new_v[:, cols] = second


def local(inputs, queries, keys, cotangent, winners, weights, first_moment, second_moment):
    f32, bf16 = jnp.float32, jnp.bfloat16
    vmem = pl.BlockSpec(memory_space=pltpu.VMEM)
    hbm = pl.BlockSpec(memory_space=pltpu.HBM)
    dma = pltpu.SemaphoreType.DMA
    scratch = [
        pltpu.VMEM((QUARTERS, PART, HEAD_DIM), bf16),
        pltpu.VMEM((PART, GROUP_HEADS * HEAD_DIM), bf16),
        pltpu.VMEM((PART, GROUP_HEADS * HEAD_DIM), bf16),
        pltpu.VMEM((PART, FEAT), bf16),
        pltpu.VMEM((FEAT, PART), bf16),
        pltpu.VMEM((QUARTERS, PART, GROUP_HEADS * PART), bf16),
        pltpu.VMEM((1, GROUP_HEADS * PART), f32),
        pltpu.VMEM((GROUP_HEADS * PART, HEAD_DIM), bf16),
        pltpu.VMEM((2, PART, HEAD_DIM), f32),
        pltpu.VMEM((3, PART, HEAD_DIM), bf16),
        pltpu.VMEM((3, PART, HEAD_DIM), bf16),
        pltpu.VMEM((2, 4 * ROWS, HEAD_DIM), f32),
        pltpu.VMEM((3, 4 * ROWS, HEAD_DIM), bf16),
        pltpu.VMEM((3, 4 * ROWS, HEAD_DIM), bf16),
        pltpu.VMEM((4 * ROWS, HEAD_DIM), bf16),
        pltpu.VMEM((4, ROWS, HEAD_DIM), bf16),
    ]
    own_state = [
        pltpu.VMEM((ROWS, KVW), bf16),
        pltpu.VMEM((ROWS, KVW), f32),
        pltpu.VMEM((ROWS, KVW), f32),
        pltpu.VMEM((8, 3 * ROWS, 128), bf16),
    ]
    landing = pltpu.VMEM((8, 3 * ROWS, 128), bf16)
    parts = []
    for rows in (48, 32, 16):
        for count in (16, SLOTS, SLOTS, 16):
            parts += [pltpu.VMEM((count, rows, 128), bf16)] * 2
    parts += [pltpu.VMEM((30, rows, 128), bf16) for rows in (48, 32, 16)]
    state_args = (weights[0], first_moment[0], second_moment[0])
    state_shape = jax.ShapeDtypeStruct((8, 3 * ROWS, 128), bf16)
    smem = pl.BlockSpec(memory_space=pltpu.SMEM)
    grad, source, flag = pl.pallas_call(
        kernel,
        out_shape=(
            jax.ShapeDtypeStruct((4, ROWS, HEAD_DIM), bf16),
            state_shape,
            jax.ShapeDtypeStruct((1,), jnp.int32),
        ),
        in_specs=[smem] + [hbm] * 7,
        out_specs=(hbm, hbm, smem),
        scratch_shapes=scratch
        + own_state
        + [landing, pltpu.VMEM((8, 128), jnp.int32), pltpu.SMEM((8, 128), jnp.int32)]
        + [dma((4,)), dma((3,)), dma((3,)), dma((4, 4)), dma((4, 4))]
        + [dma((4,))] * 4
        + [dma((2, 4)), dma((2, 4)), dma((4,)), dma((4,)), dma((6,)), dma((6,))]
        + [dma((3,)), dma((3, 2)), dma((3, 2)), dma((3, 2)), dma((3,)), dma((3,))]
        + parts,
        compiler_params=pltpu.CompilerParams(
            collective_id=0, has_side_effects=True, vmem_limit_bytes=VMEM_LIMIT
        ),
        cost_estimate=pl.CostEstimate(
            flops=3_000_000_000, bytes_accessed=6_000_000, transcendentals=4_000_000
        ),
    )(winners, inputs[0], queries[0], keys[0], cotangent[0], *state_args)

    def step(grad, source):
        return pl.pallas_call(
            adam_kernel,
            out_shape=(
                jax.ShapeDtypeStruct((ROWS, KVW), bf16),
                jax.ShapeDtypeStruct((ROWS, KVW), f32),
                jax.ShapeDtypeStruct((ROWS, KVW), f32),
            ),
            in_specs=[vmem, vmem],
            out_specs=(vmem, vmem, vmem),
            compiler_params=pltpu.CompilerParams(vmem_limit_bytes=VMEM_LIMIT),
        )(grad, source)

    def crowded():
        all_source = pl.pallas_call(
            plain_exchange,
            out_shape=state_shape,
            in_specs=[smem] + [hbm] * 3,
            out_specs=hbm,
            scratch_shapes=own_state
            + [pltpu.VMEM((MEMBERS, rows, 128), bf16) for rows in (48, 32, 16)] * 2
            + [landing, dma((3,)), dma((1,))]
            + [dma((3,))] * 4,
            compiler_params=pltpu.CompilerParams(
                collective_id=1, has_side_effects=True, vmem_limit_bytes=VMEM_LIMIT
            ),
        )(winners, *state_args)
        return step(grad, all_source)

    outs = lax.cond(flag[0] > 0, crowded, lambda: step(grad, source))
    return tuple(out[None] for out in outs)


def solution(mesh):
    rows = P("member", "fsdp", None)
    return jax.shard_map(
        local,
        mesh=mesh,
        in_specs=(rows, rows, rows, rows, P(), rows, rows, rows),
        out_specs=(rows, rows, rows),
        check_vma=False,
    )
```

```python
import jax
import jax.numpy as jnp
from jax import lax
from jax.experimental import pallas as pl
from jax.experimental.pallas import tpu as pltpu
from jax.sharding import PartitionSpec as P

MEMBERS = 32
KV_HEADS = 4
QUARTERS = 4
HEAD_DIM = 256
GROUP_HEADS = 2
TOK = 128
FEAT = 1792
X_HALF = 896
ROWS = 112
KVW = 1024
PART = QUARTERS * TOK
PIECE = 80
RING = 16
HALF = 8
SLOTS = 5
BLOCKS = 7

beta_one = 0.9
beta_two = 0.999
learning_rate = 0.001
decay_rate = 0.1
adam_eps = 1e-08
adam_step = 200
soft_cap = 50.0

VMEM_LIMIT = 60 * 1024 * 1024

MESH = pl.DeviceIdType.MESH


def kernel(
    winners, x_in, q_in, k_in, c_in, w_in, m_in, v_in,
    grad_out, source_out, flag_out, winners_out,
    k_all, q_g, c_g, x_g, x_t, expo, denom, cots,
    dv_acc, dv_out, dv_in, gr_acc, gr_out, gr_in, sum_out, grad,
    w_own, m_own, v_own, state, source, table_v, table_s,
    loc_sem, own_sem, out_sem, grp_send, grp_recv, key_send, key_recv, dv_send, dv_recv,
    gr_send, gr_recv, own_send, own_recv, x_send, x_recv, deal_send, deal_recv, swap_send, swap_recv,
    pick_send, pick_recv, *parts,
):
    me = lax.axis_index("member")
    mine = lax.axis_index("fsdp")
    dealt, swap_out, swap_in, sent = (
        [(parts[8 * part + 2 * kind], parts[8 * part + 2 * kind + 1]) for part in range(3)]
        for kind in range(4)
    )
    both = parts[24:27]
    g = mine // QUARTERS
    j = mine % QUARTERS

    sibling = j + 1 - 2 * (j % 2)
    across = (j + 2) % QUARTERS
    diagonal = (sibling + 2) % QUARTERS

    def at(quarter, head):
        return {"fsdp": head * QUARTERS + quarter}

    state_copies = [
        pltpu.make_async_copy(src, dst, own_sem.at[i])
        for i, (src, dst) in enumerate(((w_in, w_own), (m_in, m_own), (v_in, v_own)))
    ]
    for copy in state_copies:
        copy.start()

    barrier = pltpu.get_barrier_semaphore()
    for s in range(1, 4):
        pl.semaphore_signal(
            barrier, inc=1, device_id=at(j, (g + s) % 4), device_id_type=MESH
        )
        pl.semaphore_signal(
            barrier, inc=1, device_id=at((j + s) % 4, g), device_id_type=MESH
        )

    def greet(offset, row):
        pl.semaphore_signal(
            barrier,
            inc=1,
            device_id={
                "member": (me // RING + row) % 2 * RING + (me + RING + offset) % RING
            },
            device_id_type=MESH,
        )

    @pl.loop(1, 6)
    def _(s):
        for row in range(2):
            greet(s, row)
            greet(-s, row)

    greet(0, 1)

    def own_slot(kind, owner):
        rows = pl.ds(owner * TOK, TOK)
        return (k_all.at[j, rows], q_g.at[rows], c_g.at[rows], x_g.at[rows])[kind]

    def own_slice(kind, head):
        if kind == 0:
            return k_in.at[:, pl.ds(head * HEAD_DIM, HEAD_DIM)]
        if kind == 3:
            return x_in
        wide = GROUP_HEADS * HEAD_DIM
        return (q_in, c_in)[kind - 1].at[:, pl.ds(head * wide, wide)]

    def group_copy(kind, s):
        peer = (g + s) % 4
        return pltpu.make_async_remote_copy(
            src_ref=own_slice(kind, peer),
            dst_ref=own_slot(kind, g),
            send_sem=grp_send.at[kind, s],
            recv_sem=grp_recv.at[kind, s],
            device_id=at(j, peer),
            device_id_type=MESH,
        )

    def group_wait(kind):
        for s in range(1, 4):
            slot = own_slot(kind, (g + 4 - s) % 4)
            pltpu.make_async_remote_copy(
                src_ref=slot,
                dst_ref=slot,
                send_sem=grp_send.at[kind, s],
                recv_sem=grp_recv.at[kind, s],
                device_id=at(j, (g + s) % 4),
                device_id_type=MESH,
            ).wait_recv()
        local_copy(kind).wait()

    def local_copy(kind):
        return pltpu.make_async_copy(own_slice(kind, g), own_slot(kind, g), loc_sem.at[kind])

    for kind in range(4):
        local_copy(kind).start()

    pl.semaphore_wait(barrier, 6 + 21)

    for copy in state_copies:
        copy.wait()
    for band in range(8):
        cols = slice(band * 128, (band + 1) * 128)
        state[band, 0:ROWS] = w_own[:, cols]
        state[band, ROWS : 2 * ROWS] = m_own[:, cols].astype(jnp.bfloat16)
        state[band, 2 * ROWS : 3 * ROWS] = v_own[:, cols].astype(jnp.bfloat16)

    core = mine % 2
    y = me // RING
    z = me % RING
    starts, sizes = (0, 32, 80), (32, 48, 16)
    cuts = ((z + RING - 5) % RING, (z + RING - 10) % RING)
    reach = (5, 2)

    def special(r):
        return (r + 2 * core) % 4 == 1

    def has(part, r, action):
        if part < 2:
            action()
        else:
            pl.when(special(r))(action)

    def place(ref, r, part, row=None):
        piece = (y if row is None else row) * RING + r
        first = piece % 4 * PIECE + starts[part] if part < 2 else 4 * PIECE
        return ref.at[piece // 4, pl.ds(first, sizes[part])]

    def bulk(part, count, send_sem, recv_sem):
        ref = sent[part][0].at[pl.ds(0, 15)] if count == 15 else both[part].at[pl.ds(0, count)]
        return pltpu.make_async_remote_copy(
            src_ref=ref,
            dst_ref=ref,
            send_sem=send_sem,
            recv_sem=recv_sem,
            device_id={"member": (me + 1) % MEMBERS},
            device_id_type=MESH,
        )

    def in_all(part, wait):
        if part < 2:
            wait(30)
        else:
            either = special(cuts[0]) | special(cuts[1])
            pl.when(either)(lambda: wait(7))
            pl.when(jnp.logical_not(either))(lambda: wait(8))

    def deal(part):
        @pl.loop(0, HALF)
        def _(d):
            for role in range(2):
                r = (z + RING - HALF * role - d) % RING
                for row in range(2):

                    def start(role=role, row=row, r=r):
                        pltpu.make_async_remote_copy(
                            src_ref=place(state, r, part, row),
                            dst_ref=dealt[part][role].at[y * HALF + d],
                            send_sem=deal_send.at[part],
                            recv_sem=deal_recv.at[part, role],
                            device_id={
                                "member": row * RING + (z + RING + reach[role] - d) % RING
                            },
                            device_id_type=MESH,
                        ).start()

                    other = (d != reach[role]) | (y != row)
                    pl.when(other if part < 2 else other & special(r))(start)

        for role in range(2):

            def keep(role=role):
                dealt[part][role][y * HALF + reach[role]] = place(state, cuts[role], part)[...]

            has(part, cuts[role], keep)

    def seat(member, role):
        return member // RING * HALF + (member % RING + RING - cuts[role]) % HALF

    def swap_copy(part, role):
        partner = (z + 5) % RING if role == 0 else (z + RING - 5) % RING
        return pltpu.make_async_remote_copy(
            src_ref=swap_out[part][role],
            dst_ref=swap_in[part][1 - role],
            send_sem=swap_send.at[part, role],
            recv_sem=swap_recv.at[part, 1 - role],
            device_id={"member": y * RING + partner},
            device_id_type=MESH,
        )

    def swap(part):
        for role in range(2):

            def action(role=role):
                bulk(part, 15, deal_send.at[part], deal_recv.at[part, role]).wait_recv()
                for k in range(SLOTS):
                    swap_out[part][role][k] = dealt[part][role][seat(table_s[2 * role, k], role)]
                swap_copy(part, role).start()

            has(part, cuts[role], action)

    def serve(part):
        for role in range(2):

            def action(role=role):
                swap_copy(part, 1 - role).wait_recv()

                @pl.loop(0, HALF)
                def _(d):
                    for row in range(2):
                        member = row * RING + (z + RING - reach[role] + d) % RING
                        winner = winners[member]
                        inside = (winner % RING + RING - cuts[role]) % RING // HALF == role
                        near = dealt[part][role][seat(winner, role)]
                        rank = jnp.minimum(table_s[2 * role + 1, winner], SLOTS - 1)
                        far = swap_in[part][role][rank]
                        sent[part][role][row * HALF + d] = jnp.where(inside, near, far)

                        def start(row=row, member=member):
                            pltpu.make_async_remote_copy(
                                src_ref=sent[part][role].at[row * HALF + d],
                                dst_ref=place(source, cuts[role], part),
                                send_sem=pick_send.at[part],
                                recv_sem=pick_recv.at[part],
                                device_id={"member": member},
                                device_id_type=MESH,
                            ).start()

                        pl.when((d != reach[role]) | (y != row))(start)

                place(source, cuts[role], part)[...] = sent[part][role][y * HALF + reach[role]]

            has(part, cuts[role], action)

    for part in range(3):
        deal(part)

    for kind in range(3):
        for s in range(1, 4):
            group_copy(kind, s).start()

    right, left = (g + 1) % 4, (g + 3) % 4
    routes = ((0, g, right), (0, g, left), (1, g, left), (1, g, right), (0, left, right), (1, right, left))
    x_from = (left, right, right, left, left, right)
    x_owner = (left, right, right, left, (g + 2) % 4, (g + 2) % 4)

    def x_slot(owner, half):
        return x_g.at[pl.ds(owner * TOK, TOK), pl.ds(half * X_HALF, X_HALF)]

    def x_copy(route):
        half, owner, peer = routes[route]
        slot = x_slot(owner, half)
        return pltpu.make_async_remote_copy(
            src_ref=slot if route > 3 else x_in.at[:, pl.ds(half * X_HALF, X_HALF)],
            dst_ref=slot,
            send_sem=x_send.at[route],
            recv_sem=x_recv.at[route],
            device_id=at(j, peer),
            device_id_type=MESH,
        )

    def x_wait(route):
        slot = x_slot(x_owner[route], routes[route][0])
        pltpu.make_async_remote_copy(
            src_ref=slot,
            dst_ref=slot,
            send_sem=x_send.at[route],
            recv_sem=x_recv.at[route],
            device_id=at(j, x_from[route]),
            device_id_type=MESH,
        ).wait_recv()

    for route in range(4):
        x_copy(route).start()

    shape = (MEMBERS, 128)
    sub = lax.broadcasted_iota(jnp.int32, shape, 0)
    lane = lax.broadcasted_iota(jnp.int32, shape, 1)
    by_sub = jnp.zeros(shape, jnp.int32)
    by_lane = jnp.full(shape, -1, jnp.int32)
    for b in range(MEMBERS):
        by_sub = jnp.where(sub == b, winners[b], by_sub)
        by_lane = jnp.where(lane == b, winners[b], by_lane)
    one, none = jnp.ones(shape, jnp.int32), jnp.zeros(shape, jnp.int32)
    takes = jnp.where(by_lane == sub, one, none)
    taken = jnp.where(by_sub == lane, one, none)

    def inside_of(index, r, role):
        return jnp.where((index % RING + RING - r) % RING // HALF == role, one, none)

    def needed_by(r, role):
        in_sub, in_lane = inside_of(sub, r, role), inside_of(lane, r, role)
        out_sub = in_sub * jnp.max(takes * (1 - in_lane), axis=1, keepdims=True)
        return in_sub, in_lane, out_sub

    for role in range(2):
        in_sub, in_lane, out_sub = needed_by(cuts[role], role)
        out_lane = in_lane * jnp.max(taken * (1 - in_sub), axis=0, keepdims=True)
        rank = jnp.sum(jnp.where(lane < sub, out_lane, none), axis=1, keepdims=True)
        chosen = jnp.where(rank == lane, out_sub * sub, none)
        table_v[2 * role : 2 * role + 1, :] = jnp.sum(chosen, axis=0, keepdims=True)
        in_need = (1 - in_sub) * jnp.max(takes * in_lane, axis=1, keepdims=True)
        table_v[2 * role + 1 : 2 * role + 2, :] = jnp.sum(
            jnp.where(sub < lane, in_need, none), axis=0, keepdims=True
        )
    table_copy = pltpu.make_async_copy(table_v, table_s, out_sem.at[2])
    table_copy.start()

    most = jnp.zeros((1, 128), jnp.int32)
    for r in range(RING):
        most = jnp.maximum(most, jnp.sum(needed_by(r, 0)[2], axis=0, keepdims=True))
    flag_out[0] = jnp.max(jnp.where(most > SLOTS, 1, 0))

    @pl.loop(0, MEMBERS)
    def _(b):
        winners_out[b] = winners[b]

    table_copy.wait()

    def key_copy(route):
        slot = k_all.at[across if route == 2 else j]
        return pltpu.make_async_remote_copy(
            src_ref=slot,
            dst_ref=slot,
            send_sem=key_send.at[route],
            recv_sem=key_recv.at[route],
            device_id=at(across if route == 1 else sibling, g),
            device_id_type=MESH,
        )

    def key_wait(route):
        slot = k_all.at[(sibling, across, diagonal)[route]]
        pltpu.make_async_remote_copy(
            src_ref=slot,
            dst_ref=slot,
            send_sem=key_send.at[route],
            recv_sem=key_recv.at[route],
            device_id=at(across if route == 1 else sibling, g),
            device_id_type=MESH,
        ).wait_recv()

    group_wait(0)
    key_copy(1).start()
    key_copy(0).start()

    swap(0)
    group_wait(1)
    denom[...] = jnp.zeros_like(denom)

    def scores(chunk):
        later = jnp.where(chunk > j, TOK, jnp.where(chunk < j, -TOK, 0))
        for i in range(4):
            first = i * TOK
            key_block = k_all[chunk, first : first + TOK, :]
            for h in range(GROUP_HEADS):
                raw = lax.dot_general(
                    key_block,
                    q_g[first:PART, h * HEAD_DIM : (h + 1) * HEAD_DIM],
                    (((1,), (1,)), ((), ())),
                    preferred_element_type=jnp.float32,
                )
                e = jnp.exp(soft_cap * jnp.tanh(raw * (HEAD_DIM**-0.5 / soft_cap)))
                u = lax.broadcasted_iota(jnp.int32, raw.shape, 0)
                t = lax.broadcasted_iota(jnp.int32, raw.shape, 1)
                e = jnp.where((u + later <= t) | (t >= TOK), e, 0.0)
                cols = slice(h * PART + first, (h + 1) * PART)
                expo[chunk, first : first + TOK, cols] = e.astype(jnp.bfloat16)
                denom[:, cols] += jnp.sum(e, axis=0, keepdims=True)

    scores(j)

    key_wait(1)
    key_copy(2).start()
    key_wait(0)

    @pl.loop(0, 3)
    def _(s):
        pl.when(s == 2)(lambda: key_wait(2))
        scores(jnp.where(s == 0, sibling, jnp.where(s == 1, across, diagonal)))

    swap(1)
    swap(2)

    group_wait(2)
    for h in range(GROUP_HEADS):
        cols = slice(h * PART, (h + 1) * PART)
        inverse = jnp.transpose(jnp.broadcast_to(1.0 / denom[:, cols], (128, PART)))
        heads = c_g[:, h * HEAD_DIM : (h + 1) * HEAD_DIM].astype(jnp.float32)
        for half in range(2):
            lanes = slice(half * 128, (half + 1) * 128)
            cots[cols, lanes] = (heads[:, lanes] * inverse).astype(jnp.bfloat16)

    def dv_copy(slot):
        return pltpu.make_async_remote_copy(
            src_ref=dv_out.at[slot],
            dst_ref=dv_in.at[slot],
            send_sem=dv_send.at[slot],
            recv_sem=dv_recv.at[slot],
            device_id=at(across if slot == 2 else sibling, g),
            device_id_type=MESH,
        )

    def dv_rows(chunk, i):
        first = i * TOK
        total = None
        for h in range(GROUP_HEADS):
            cols = slice(h * PART + first, (h + 1) * PART)
            term = jnp.dot(
                expo[chunk, first : first + TOK, cols],
                cots[cols, :],
                preferred_element_type=jnp.float32,
            )
            total = term if total is None else total + term
        return total

    for slot, chunk in ((1, diagonal), (0, sibling)):
        for i in range(4):
            dv_out[slot, i * TOK : (i + 1) * TOK] = dv_rows(chunk, i).astype(jnp.bfloat16)
        dv_copy(slot).start()

    @pl.loop(0, 2)
    def _(step):
        chunk = jnp.where(step == 0, across, j)
        for i in range(4):
            dv_acc[step, i * TOK : (i + 1) * TOK] = dv_rows(chunk, i)

    dv_copy(1).wait_recv()
    dv_out[2] = (dv_acc[0] + dv_in[1].astype(jnp.float32)).astype(jnp.bfloat16)
    dv_copy(2).start()

    serve(0)

    x_wait(0)
    x_copy(4).start()
    x_wait(2)
    x_copy(5).start()

    serve(1)
    serve(2)

    local_copy(3).wait()

    def turn(half):
        for route in ((1, 4), (3, 5))[half]:
            x_wait(route)

        @pl.loop(0, X_HALF // 128)
        def _(i):
            first = pl.multiple_of(half * X_HALF + i * 128, 128)
            x_t[pl.ds(first, 128), :] = jnp.transpose(x_g[:, pl.ds(first, 128)])

    turn(0)

    dv_copy(0).wait_recv()
    dv_copy(2).wait_recv()
    dv_low = (
        dv_acc[1] + dv_in[0].astype(jnp.float32) + dv_in[2].astype(jnp.float32)
    ).astype(jnp.bfloat16)

    def gr_copy(slot, half):
        rows = pl.ds(half * 2 * ROWS, 2 * ROWS)
        return pltpu.make_async_remote_copy(
            src_ref=gr_out.at[slot, rows],
            dst_ref=gr_in.at[slot, rows],
            send_sem=gr_send.at[half, slot],
            recv_sem=gr_recv.at[half, slot],
            device_id=at(across if slot == 2 else sibling, g),
            device_id_type=MESH,
        )

    def rows_of(quarter, i):
        first = pl.multiple_of((i * QUARTERS + quarter) * ROWS, 16)
        return jnp.dot(x_t[pl.ds(first, ROWS), :], dv_low, preferred_element_type=jnp.float32)

    def spread(half):
        blocks = (2 * half, 2 * half + 1)
        rows = slice(half * 2 * ROWS, (half + 1) * 2 * ROWS)
        for slot, quarter in ((1, diagonal), (0, sibling)):
            for i in blocks:
                gr_out[slot, i * ROWS : (i + 1) * ROWS] = rows_of(quarter, i).astype(jnp.bfloat16)
            gr_copy(slot, half).start()
        for slot, quarter in ((0, across), (1, j)):
            for i in blocks:
                gr_acc[slot, i * ROWS : (i + 1) * ROWS] = rows_of(quarter, i)
        gr_copy(1, half).wait_recv()
        gr_out[2, rows] = (gr_acc[0, rows] + gr_in[1, rows].astype(jnp.float32)).astype(
            jnp.bfloat16
        )
        gr_copy(2, half).start()

    def own_copy(i):
        return pltpu.make_async_remote_copy(
            src_ref=sum_out.at[pl.ds(i * ROWS, ROWS)],
            dst_ref=grad.at[g],
            send_sem=own_send.at[i],
            recv_sem=own_recv.at[g],
            device_id=at(j, i),
            device_id_type=MESH,
        )

    def deliver(half):
        rows = slice(half * 2 * ROWS, (half + 1) * 2 * ROWS)
        total = gr_acc[1, rows]
        for slot in (0, 2):
            gr_copy(slot, half).wait_recv()
            total += gr_in[slot, rows].astype(jnp.float32)
        sum_out[rows] = total.astype(jnp.bfloat16)
        for i in (2 * half, 2 * half + 1):
            pl.when(g != i)(lambda: own_copy(i).start())

            @pl.when(g == i)
            def _(i=i):
                grad[i] = sum_out[i * ROWS : (i + 1) * ROWS]

    spread(0)
    turn(1)
    spread(1)
    deliver(0)
    deliver(1)

    for s in range(1, 4):
        peer = (g + s) % 4
        slot = grad.at[peer]
        pltpu.make_async_remote_copy(
            src_ref=slot,
            dst_ref=slot,
            send_sem=own_send.at[peer],
            recv_sem=own_recv.at[peer],
            device_id=at(j, peer),
            device_id_type=MESH,
        ).wait_recv()

    grad_copy = pltpu.make_async_copy(grad, grad_out, out_sem.at[0])
    grad_copy.start()

    for part in range(3):
        in_all(
            part,
            lambda n: bulk(part, n, deal_send.at[part], pick_recv.at[part]).wait_send(),
        )
        for role in range(2):
            has(part, cuts[role], lambda: swap_copy(part, role).wait_send())
    for part in range(3):
        in_all(
            part,
            lambda n: bulk(part, n, deal_send.at[part], pick_recv.at[part]).wait_recv(),
        )

    source_copy = pltpu.make_async_copy(source, source_out, out_sem.at[1])
    source_copy.start()

    for s in range(1, 4):
        for kind in range(3):
            group_copy(kind, s).wait_send()

        key_copy(s - 1).wait_send()
        dv_copy(s - 1).wait_send()
        gr_copy(s - 1, 0).wait_send()
        gr_copy(s - 1, 1).wait_send()
        own_copy((g + s) % 4).wait_send()
    for route in range(6):
        x_copy(route).wait_send()

    for part in range(3):
        for role in range(2):
            has(
                part,
                cuts[role],
                lambda: bulk(part, 15, pick_send.at[part], pick_recv.at[part]).wait_send(),
            )

    grad_copy.wait()
    source_copy.wait()


def plain_exchange(
    winners, w_in, m_in, v_in, source_out,
    w_own, m_own, v_own, state, dealt_0, dealt_1, dealt_2, picked_0, picked_1, picked_2, source,
    own_sem, out_sem, deal_send, deal_recv, pick_send, pick_recv,
):
    me = lax.axis_index("member")
    mine = lax.axis_index("fsdp")

    state_copies = [
        pltpu.make_async_copy(src, dst, own_sem.at[i])
        for i, (src, dst) in enumerate(((w_in, w_own), (m_in, m_own), (v_in, v_own)))
    ]
    for copy in state_copies:
        copy.start()

    barrier = pltpu.get_barrier_semaphore()

    @pl.loop(1, MEMBERS)
    def _(s):
        pl.semaphore_signal(
            barrier, inc=1, device_id={"member": (me + s) % MEMBERS}, device_id_type=MESH
        )

    for copy in state_copies:
        copy.wait()
    for band in range(8):
        cols = slice(band * 128, (band + 1) * 128)
        state[band, 0:ROWS] = w_own[:, cols]
        state[band, ROWS : 2 * ROWS] = m_own[:, cols].astype(jnp.bfloat16)
        state[band, 2 * ROWS : 3 * ROWS] = v_own[:, cols].astype(jnp.bfloat16)
    pl.semaphore_wait(barrier, MEMBERS - 1)

    core = mine % 2
    starts, sizes = (0, 48, 80), (48, 32, 16)
    dealt, picked = (dealt_0, dealt_1, dealt_2), (picked_0, picked_1, picked_2)

    def extra(member):
        return (member + 2 * core) % 4 == 1

    def sorts(member, part, action):
        if part < 2:
            action()
        else:
            pl.when(extra(member))(action)

    def place(ref, member, part):
        first = member % 4 * PIECE + starts[part] if part < 2 else 4 * PIECE
        return ref.at[member // 4, pl.ds(first, sizes[part])]

    def deal_copy(s, part):
        peer = (me + s) % MEMBERS
        return pltpu.make_async_remote_copy(
            src_ref=place(state, peer, part),
            dst_ref=dealt[part].at[me],
            send_sem=deal_send.at[part],
            recv_sem=deal_recv.at[part],
            device_id={"member": peer},
            device_id_type=MESH,
        )

    def all_of(part, count, send_sem, recv_sem):
        ref = dealt[part].at[pl.ds(0, count)]
        return pltpu.make_async_remote_copy(
            src_ref=ref,
            dst_ref=ref,
            send_sem=send_sem.at[part],
            recv_sem=recv_sem.at[part],
            device_id={"member": (me + 1) % MEMBERS},
            device_id_type=MESH,
        )

    def to_or_from_sorters(part, wait):
        if part < 2:
            wait(MEMBERS - 1)
        else:
            pl.when(extra(me))(lambda: wait(MEMBERS // 4 - 1))
            pl.when(jnp.logical_not(extra(me)))(lambda: wait(MEMBERS // 4))

    for part in range(3):

        @pl.loop(1, MEMBERS)
        def _(s):
            sorts((me + s) % MEMBERS, part, lambda: deal_copy(s, part).start())

    def keep(part):
        dealt[part][me] = place(state, me, part)[...]

    for part in range(3):
        sorts(me, part, lambda: keep(part))

    def pick_copy(s, part):
        peer = (me + s) % MEMBERS
        return pltpu.make_async_remote_copy(
            src_ref=picked[part].at[s],
            dst_ref=place(source, me, part),
            send_sem=pick_send.at[part],
            recv_sem=pick_recv.at[part],
            device_id={"member": peer},
            device_id_type=MESH,
        )

    def pick(part):
        def action():
            all_of(part, MEMBERS - 1, deal_send, deal_recv).wait_recv()

            @pl.loop(1, MEMBERS)
            def _(s):
                picked[part][s] = dealt[part][winners[(me + s) % MEMBERS]]
                pick_copy(s, part).start()

            place(source, me, part)[...] = dealt[part][winners[me]]

        sorts(me, part, action)

    for part in range(3):
        pick(part)
    for part in range(3):
        to_or_from_sorters(
            part, lambda count: all_of(part, count, deal_send, deal_recv).wait_send()
        )
    for part in range(3):
        to_or_from_sorters(
            part, lambda count: all_of(part, count, pick_send, pick_recv).wait_recv()
        )

    source_copy = pltpu.make_async_copy(source, source_out, out_sem.at[0])
    source_copy.start()
    for part in range(3):
        sorts(
            me, part, lambda: all_of(part, MEMBERS - 1, pick_send, pick_recv).wait_send()
        )
    source_copy.wait()


def adam_kernel(grad, source, new_w, new_m, new_v):
    for band in range(8):
        cols = slice(band * 128, (band + 1) * 128)
        lanes = slice(band % 2 * 128, band % 2 * 128 + 128)
        gradient = grad[band // 2, :, lanes].astype(jnp.float32)
        old_w = source[band, 0:ROWS].astype(jnp.float32)
        old_m = source[band, ROWS : 2 * ROWS].astype(jnp.float32)
        old_v = source[band, 2 * ROWS : 3 * ROWS].astype(jnp.float32)
        first = beta_one * old_m + (1.0 - beta_one) * gradient
        second = beta_two * old_v + (1.0 - beta_two) * gradient * gradient
        first_hat = first * (1.0 / (1.0 - beta_one**adam_step))
        second_hat = second * (1.0 / (1.0 - beta_two**adam_step))
        update = first_hat / (jnp.sqrt(second_hat) + adam_eps) + decay_rate * old_w
        new_w[:, cols] = (old_w - learning_rate * update).astype(jnp.bfloat16)
        new_m[:, cols] = first
        new_v[:, cols] = second


def local(inputs, queries, keys, cotangent, winners, weights, first_moment, second_moment):
    f32, bf16 = jnp.float32, jnp.bfloat16
    vmem = pl.BlockSpec(memory_space=pltpu.VMEM)
    hbm = pl.BlockSpec(memory_space=pltpu.HBM)
    dma = pltpu.SemaphoreType.DMA
    scratch = [
        pltpu.VMEM((QUARTERS, PART, HEAD_DIM), bf16),
        pltpu.VMEM((PART, GROUP_HEADS * HEAD_DIM), bf16),
        pltpu.VMEM((PART, GROUP_HEADS * HEAD_DIM), bf16),
        pltpu.VMEM((PART, FEAT), bf16),
        pltpu.VMEM((FEAT, PART), bf16),
        pltpu.VMEM((QUARTERS, PART, GROUP_HEADS * PART), bf16),
        pltpu.VMEM((1, GROUP_HEADS * PART), f32),
        pltpu.VMEM((GROUP_HEADS * PART, HEAD_DIM), bf16),
        pltpu.VMEM((2, PART, HEAD_DIM), f32),
        pltpu.VMEM((3, PART, HEAD_DIM), bf16),
        pltpu.VMEM((3, PART, HEAD_DIM), bf16),
        pltpu.VMEM((2, 4 * ROWS, HEAD_DIM), f32),
        pltpu.VMEM((3, 4 * ROWS, HEAD_DIM), bf16),
        pltpu.VMEM((3, 4 * ROWS, HEAD_DIM), bf16),
        pltpu.VMEM((4 * ROWS, HEAD_DIM), bf16),
        pltpu.VMEM((4, ROWS, HEAD_DIM), bf16),
    ]
    own_state = [
        pltpu.VMEM((ROWS, KVW), bf16),
        pltpu.VMEM((ROWS, KVW), f32),
        pltpu.VMEM((ROWS, KVW), f32),
        pltpu.VMEM((8, 3 * ROWS, 128), bf16),
    ]
    landing = pltpu.VMEM((8, 3 * ROWS, 128), bf16)
    parts = []
    for rows in (32, 48, 16):
        for count in (16, SLOTS, SLOTS, 16):
            parts += [pltpu.VMEM((count, rows, 128), bf16)] * 2
    parts += [pltpu.VMEM((30, rows, 128), bf16) for rows in (32, 48, 16)]
    state_args = (weights[0], first_moment[0], second_moment[0])
    state_shape = jax.ShapeDtypeStruct((8, 3 * ROWS, 128), bf16)
    smem = pl.BlockSpec(memory_space=pltpu.SMEM)
    grad, source, flag, same_winners = pl.pallas_call(
        kernel,
        out_shape=(
            jax.ShapeDtypeStruct((4, ROWS, HEAD_DIM), bf16),
            state_shape,
            jax.ShapeDtypeStruct((1,), jnp.int32),
            jax.ShapeDtypeStruct((MEMBERS,), jnp.int32),
        ),
        in_specs=[smem] + [hbm] * 7,
        out_specs=(hbm, hbm, smem, smem),
        scratch_shapes=scratch
        + own_state
        + [landing, pltpu.VMEM((8, 128), jnp.int32), pltpu.SMEM((8, 128), jnp.int32)]
        + [dma((4,)), dma((3,)), dma((3,)), dma((4, 4)), dma((4, 4))]
        + [dma((4,))] * 4
        + [dma((2, 4)), dma((2, 4)), dma((4,)), dma((4,)), dma((6,)), dma((6,))]
        + [dma((3,)), dma((3, 2)), dma((3, 2)), dma((3, 2)), dma((3,)), dma((3,))]
        + parts,
        compiler_params=pltpu.CompilerParams(
            collective_id=0, has_side_effects=True, vmem_limit_bytes=VMEM_LIMIT
        ),
        cost_estimate=pl.CostEstimate(
            flops=3_000_000_000, bytes_accessed=6_000_000, transcendentals=4_000_000
        ),
    )(winners, inputs[0], queries[0], keys[0], cotangent[0], *state_args)

    def step(grad, source):
        return pl.pallas_call(
            adam_kernel,
            out_shape=(
                jax.ShapeDtypeStruct((ROWS, KVW), bf16),
                jax.ShapeDtypeStruct((ROWS, KVW), f32),
                jax.ShapeDtypeStruct((ROWS, KVW), f32),
            ),
            in_specs=[vmem, vmem],
            out_specs=(vmem, vmem, vmem),
            compiler_params=pltpu.CompilerParams(vmem_limit_bytes=VMEM_LIMIT),
        )(grad, source)

    def crowded():
        all_source = pl.pallas_call(
            plain_exchange,
            out_shape=state_shape,
            in_specs=[smem] + [hbm] * 3,
            out_specs=hbm,
            scratch_shapes=own_state
            + [pltpu.VMEM((MEMBERS, rows, 128), bf16) for rows in (48, 32, 16)] * 2
            + [landing, dma((3,)), dma((1,))]
            + [dma((3,))] * 4,
            compiler_params=pltpu.CompilerParams(
                collective_id=1, has_side_effects=True, vmem_limit_bytes=VMEM_LIMIT
            ),
        )(same_winners, *state_args)
        return step(grad, all_source)

    outs = lax.cond(flag[0] > 0, crowded, lambda: step(grad, source))
    return tuple(out[None] for out in outs)


def solution(mesh):
    rows = P("member", "fsdp", None)
    return jax.shard_map(
        local,
        mesh=mesh,
        in_specs=(rows, rows, rows, rows, P(), rows, rows, rows),
        out_specs=(rows, rows, rows),
        check_vma=False,
    )
```

```python
import jax
import jax.numpy as jnp
from jax import lax
from jax.experimental import pallas as pl
from jax.experimental.pallas import tpu as pltpu
from jax.sharding import PartitionSpec as P

MEMBERS = 32
KV_HEADS = 4
QUARTERS = 4
HEAD_DIM = 256
GROUP_HEADS = 2
TOK = 128
FEAT = 1792
X_HALF = 896
ROWS = 112
KVW = 1024
PART = QUARTERS * TOK
PIECE = 80
RING = 16
HALF = 8
SLOTS = 5
BLOCKS = 7

beta_one = 0.9
beta_two = 0.999
learning_rate = 0.001
decay_rate = 0.1
adam_eps = 1e-08
adam_step = 200
soft_cap = 50.0

VMEM_LIMIT = 60 * 1024 * 1024

MESH = pl.DeviceIdType.MESH


def kernel(
    winners, x_in, q_in, k_in, c_in, w_in, m_in, v_in,
    grad_out, source_out, flag_out, winners_out,
    k_all, q_g, c_g, x_g, x_t, expo, denom, cots,
    dv_acc, dv_out, dv_in, gr_acc, gr_out, gr_in, sum_out, grad,
    w_own, m_own, v_own, state, source, table_v, table_s,
    loc_sem, own_sem, out_sem, grp_send, grp_recv, key_send, key_recv, dv_send, dv_recv,
    gr_send, gr_recv, own_send, own_recv, x_send, x_recv, deal_send, deal_recv, swap_send, swap_recv,
    pick_send, pick_recv, *parts,
):
    me = lax.axis_index("member")
    mine = lax.axis_index("fsdp")
    dealt, swap_out, swap_in, sent = (
        [(parts[8 * part + 2 * kind], parts[8 * part + 2 * kind + 1]) for part in range(3)]
        for kind in range(4)
    )
    both = parts[24:27]
    g = mine // QUARTERS
    j = mine % QUARTERS

    sibling = j + 1 - 2 * (j % 2)
    across = (j + 2) % QUARTERS
    diagonal = (sibling + 2) % QUARTERS

    def at(quarter, head):
        return {"fsdp": head * QUARTERS + quarter}

    state_copies = [
        pltpu.make_async_copy(src, dst, own_sem.at[i])
        for i, (src, dst) in enumerate(((w_in, w_own), (m_in, m_own), (v_in, v_own)))
    ]
    for copy in state_copies:
        copy.start()

    barrier = pltpu.get_barrier_semaphore()
    for s in range(1, 4):
        pl.semaphore_signal(
            barrier, inc=1, device_id=at(j, (g + s) % 4), device_id_type=MESH
        )
        pl.semaphore_signal(
            barrier, inc=1, device_id=at((j + s) % 4, g), device_id_type=MESH
        )

    def greet(offset, row):
        pl.semaphore_signal(
            barrier,
            inc=1,
            device_id={
                "member": (me // RING + row) % 2 * RING + (me + RING + offset) % RING
            },
            device_id_type=MESH,
        )

    @pl.loop(1, 6)
    def _(s):
        for row in range(2):
            greet(s, row)
            greet(-s, row)

    greet(0, 1)

    def own_slot(kind, owner):
        rows = pl.ds(owner * TOK, TOK)
        return (k_all.at[j, rows], q_g.at[rows], c_g.at[rows], x_g.at[rows])[kind]

    def own_slice(kind, head):
        if kind == 0:
            return k_in.at[:, pl.ds(head * HEAD_DIM, HEAD_DIM)]
        if kind == 3:
            return x_in
        wide = GROUP_HEADS * HEAD_DIM
        return (q_in, c_in)[kind - 1].at[:, pl.ds(head * wide, wide)]

    def group_copy(kind, s):
        peer = (g + s) % 4
        return pltpu.make_async_remote_copy(
            src_ref=own_slice(kind, peer),
            dst_ref=own_slot(kind, g),
            send_sem=grp_send.at[kind, s],
            recv_sem=grp_recv.at[kind, s],
            device_id=at(j, peer),
            device_id_type=MESH,
        )

    def group_wait(kind):
        for s in range(1, 4):
            slot = own_slot(kind, (g + 4 - s) % 4)
            pltpu.make_async_remote_copy(
                src_ref=slot,
                dst_ref=slot,
                send_sem=grp_send.at[kind, s],
                recv_sem=grp_recv.at[kind, s],
                device_id=at(j, (g + s) % 4),
                device_id_type=MESH,
            ).wait_recv()
        local_copy(kind).wait()

    def local_copy(kind):
        return pltpu.make_async_copy(own_slice(kind, g), own_slot(kind, g), loc_sem.at[kind])

    for kind in range(4):
        local_copy(kind).start()

    pl.semaphore_wait(barrier, 6 + 21)

    for copy in state_copies:
        copy.wait()
    for band in range(8):
        cols = slice(band * 128, (band + 1) * 128)
        state[band, 0:ROWS] = w_own[:, cols]
        state[band, ROWS : 2 * ROWS] = m_own[:, cols].astype(jnp.bfloat16)
        state[band, 2 * ROWS : 3 * ROWS] = v_own[:, cols].astype(jnp.bfloat16)

    core = mine % 2
    y = me // RING
    z = me % RING
    starts, sizes = (0, 32, 80), (32, 48, 16)
    cuts = ((z + RING - 5) % RING, (z + RING - 10) % RING)
    reach = (5, 2)

    def special(r):
        return (r + 2 * core) % 4 == 1

    def has(part, r, action):
        if part < 2:
            action()
        else:
            pl.when(special(r))(action)

    def place(ref, r, part, row=None):
        piece = (y if row is None else row) * RING + r
        first = piece % 4 * PIECE + starts[part] if part < 2 else 4 * PIECE
        return ref.at[piece // 4, pl.ds(first, sizes[part])]

    def bulk(part, count, send_sem, recv_sem):
        ref = sent[part][0].at[pl.ds(0, 15)] if count == 15 else both[part].at[pl.ds(0, count)]
        return pltpu.make_async_remote_copy(
            src_ref=ref,
            dst_ref=ref,
            send_sem=send_sem,
            recv_sem=recv_sem,
            device_id={"member": (me + 1) % MEMBERS},
            device_id_type=MESH,
        )

    def in_all(part, wait):
        if part < 2:
            wait(30)
        else:
            either = special(cuts[0]) | special(cuts[1])
            pl.when(either)(lambda: wait(7))
            pl.when(jnp.logical_not(either))(lambda: wait(8))

    def deal(part):
        @pl.loop(0, HALF)
        def _(step):
            for role in range(2):
                d = step if role == 0 else HALF - 1 - step
                r = (z + RING - HALF * role - d) % RING
                for row in range(2):

                    def start(role=role, row=row, r=r, d=d):
                        pltpu.make_async_remote_copy(
                            src_ref=place(state, r, part, row),
                            dst_ref=dealt[part][role].at[y * HALF + d],
                            send_sem=deal_send.at[part],
                            recv_sem=deal_recv.at[part, role],
                            device_id={
                                "member": row * RING + (z + RING + reach[role] - d) % RING
                            },
                            device_id_type=MESH,
                        ).start()

                    other = (d != reach[role]) | (y != row)
                    pl.when(other if part < 2 else other & special(r))(start)

        for role in range(2):

            def keep(role=role):
                dealt[part][role][y * HALF + reach[role]] = place(state, cuts[role], part)[...]

            has(part, cuts[role], keep)

    def seat(member, role):
        return member // RING * HALF + (member % RING + RING - cuts[role]) % HALF

    def swap_copy(part, role):
        partner = (z + 5) % RING if role == 0 else (z + RING - 5) % RING
        return pltpu.make_async_remote_copy(
            src_ref=swap_out[part][role],
            dst_ref=swap_in[part][1 - role],
            send_sem=swap_send.at[part, role],
            recv_sem=swap_recv.at[part, 1 - role],
            device_id={"member": y * RING + partner},
            device_id_type=MESH,
        )

    def swap(part):
        for role in range(2):

            def action(role=role):
                bulk(part, 15, deal_send.at[part], deal_recv.at[part, role]).wait_recv()
                for k in range(SLOTS):
                    swap_out[part][role][k] = dealt[part][role][seat(table_s[2 * role, k], role)]
                swap_copy(part, role).start()

            has(part, cuts[role], action)

    def serve(part):
        for role in range(2):

            def action(role=role):
                swap_copy(part, 1 - role).wait_recv()

                @pl.loop(0, HALF)
                def _(step):
                    d = step if role == 0 else HALF - 1 - step
                    for row in range(2):
                        member = row * RING + (z + RING - reach[role] + d) % RING
                        winner = winners[member]
                        inside = (winner % RING + RING - cuts[role]) % RING // HALF == role
                        near = dealt[part][role][seat(winner, role)]
                        rank = jnp.minimum(table_s[2 * role + 1, winner], SLOTS - 1)
                        far = swap_in[part][role][rank]
                        sent[part][role][row * HALF + d] = jnp.where(inside, near, far)

                        def start(row=row, member=member):
                            pltpu.make_async_remote_copy(
                                src_ref=sent[part][role].at[row * HALF + d],
                                dst_ref=place(source, cuts[role], part),
                                send_sem=pick_send.at[part],
                                recv_sem=pick_recv.at[part],
                                device_id={"member": member},
                                device_id_type=MESH,
                            ).start()

                        pl.when((d != reach[role]) | (y != row))(start)

                place(source, cuts[role], part)[...] = sent[part][role][y * HALF + reach[role]]

            has(part, cuts[role], action)

    for part in range(3):
        deal(part)

    for kind in range(3):
        for s in range(1, 4):
            group_copy(kind, s).start()

    right, left = (g + 1) % 4, (g + 3) % 4
    routes = ((0, g, right), (0, g, left), (1, g, left), (1, g, right), (0, left, right), (1, right, left))
    x_from = (left, right, right, left, left, right)
    x_owner = (left, right, right, left, (g + 2) % 4, (g + 2) % 4)

    def x_slot(owner, half):
        return x_g.at[pl.ds(owner * TOK, TOK), pl.ds(half * X_HALF, X_HALF)]

    def x_copy(route):
        half, owner, peer = routes[route]
        slot = x_slot(owner, half)
        return pltpu.make_async_remote_copy(
            src_ref=slot if route > 3 else x_in.at[:, pl.ds(half * X_HALF, X_HALF)],
            dst_ref=slot,
            send_sem=x_send.at[route],
            recv_sem=x_recv.at[route],
            device_id=at(j, peer),
            device_id_type=MESH,
        )

    def x_wait(route):
        slot = x_slot(x_owner[route], routes[route][0])
        pltpu.make_async_remote_copy(
            src_ref=slot,
            dst_ref=slot,
            send_sem=x_send.at[route],
            recv_sem=x_recv.at[route],
            device_id=at(j, x_from[route]),
            device_id_type=MESH,
        ).wait_recv()

    for route in range(4):
        x_copy(route).start()

    shape = (MEMBERS, 128)
    sub = lax.broadcasted_iota(jnp.int32, shape, 0)
    lane = lax.broadcasted_iota(jnp.int32, shape, 1)
    by_sub = jnp.zeros(shape, jnp.int32)
    by_lane = jnp.full(shape, -1, jnp.int32)
    for b in range(MEMBERS):
        by_sub = jnp.where(sub == b, winners[b], by_sub)
        by_lane = jnp.where(lane == b, winners[b], by_lane)
    one, none = jnp.ones(shape, jnp.int32), jnp.zeros(shape, jnp.int32)
    takes = jnp.where(by_lane == sub, one, none)
    taken = jnp.where(by_sub == lane, one, none)

    def inside_of(index, r, role):
        return jnp.where((index % RING + RING - r) % RING // HALF == role, one, none)

    def needed_by(r, role):
        in_sub, in_lane = inside_of(sub, r, role), inside_of(lane, r, role)
        out_sub = in_sub * jnp.max(takes * (1 - in_lane), axis=1, keepdims=True)
        return in_sub, in_lane, out_sub

    for role in range(2):
        in_sub, in_lane, out_sub = needed_by(cuts[role], role)
        out_lane = in_lane * jnp.max(taken * (1 - in_sub), axis=0, keepdims=True)
        rank = jnp.sum(jnp.where(lane < sub, out_lane, none), axis=1, keepdims=True)
        chosen = jnp.where(rank == lane, out_sub * sub, none)
        table_v[2 * role : 2 * role + 1, :] = jnp.sum(chosen, axis=0, keepdims=True)
        in_need = (1 - in_sub) * jnp.max(takes * in_lane, axis=1, keepdims=True)
        table_v[2 * role + 1 : 2 * role + 2, :] = jnp.sum(
            jnp.where(sub < lane, in_need, none), axis=0, keepdims=True
        )
    table_copy = pltpu.make_async_copy(table_v, table_s, out_sem.at[2])
    table_copy.start()

    most = jnp.zeros((1, 128), jnp.int32)
    for r in range(RING):
        most = jnp.maximum(most, jnp.sum(needed_by(r, 0)[2], axis=0, keepdims=True))
    flag_out[0] = jnp.max(jnp.where(most > SLOTS, 1, 0))

    @pl.loop(0, MEMBERS)
    def _(b):
        winners_out[b] = winners[b]

    table_copy.wait()

    def key_copy(route):
        slot = k_all.at[across if route == 2 else j]
        return pltpu.make_async_remote_copy(
            src_ref=slot,
            dst_ref=slot,
            send_sem=key_send.at[route],
            recv_sem=key_recv.at[route],
            device_id=at(across if route == 1 else sibling, g),
            device_id_type=MESH,
        )

    def key_wait(route):
        slot = k_all.at[(sibling, across, diagonal)[route]]
        pltpu.make_async_remote_copy(
            src_ref=slot,
            dst_ref=slot,
            send_sem=key_send.at[route],
            recv_sem=key_recv.at[route],
            device_id=at(across if route == 1 else sibling, g),
            device_id_type=MESH,
        ).wait_recv()

    group_wait(0)
    key_copy(1).start()
    key_copy(0).start()

    swap(0)
    group_wait(1)
    denom[...] = jnp.zeros_like(denom)

    def scores(chunk):
        later = jnp.where(chunk > j, TOK, jnp.where(chunk < j, -TOK, 0))
        for i in range(4):
            first = i * TOK
            key_block = k_all[chunk, first : first + TOK, :]
            for h in range(GROUP_HEADS):
                raw = lax.dot_general(
                    key_block,
                    q_g[first:PART, h * HEAD_DIM : (h + 1) * HEAD_DIM],
                    (((1,), (1,)), ((), ())),
                    preferred_element_type=jnp.float32,
                )
                e = jnp.exp(soft_cap * jnp.tanh(raw * (HEAD_DIM**-0.5 / soft_cap)))
                u = lax.broadcasted_iota(jnp.int32, raw.shape, 0)
                t = lax.broadcasted_iota(jnp.int32, raw.shape, 1)
                e = jnp.where((u + later <= t) | (t >= TOK), e, 0.0)
                cols = slice(h * PART + first, (h + 1) * PART)
                expo[chunk, first : first + TOK, cols] = e.astype(jnp.bfloat16)
                denom[:, cols] += jnp.sum(e, axis=0, keepdims=True)

    scores(j)

    key_wait(1)
    key_copy(2).start()
    key_wait(0)

    @pl.loop(0, 3)
    def _(s):
        pl.when(s == 2)(lambda: key_wait(2))
        scores(jnp.where(s == 0, sibling, jnp.where(s == 1, across, diagonal)))

    swap(1)
    swap(2)

    group_wait(2)
    for h in range(GROUP_HEADS):
        cols = slice(h * PART, (h + 1) * PART)
        inverse = jnp.transpose(jnp.broadcast_to(1.0 / denom[:, cols], (128, PART)))
        heads = c_g[:, h * HEAD_DIM : (h + 1) * HEAD_DIM].astype(jnp.float32)
        for half in range(2):
            lanes = slice(half * 128, (half + 1) * 128)
            cots[cols, lanes] = (heads[:, lanes] * inverse).astype(jnp.bfloat16)

    def dv_copy(slot):
        return pltpu.make_async_remote_copy(
            src_ref=dv_out.at[slot],
            dst_ref=dv_in.at[slot],
            send_sem=dv_send.at[slot],
            recv_sem=dv_recv.at[slot],
            device_id=at(across if slot == 2 else sibling, g),
            device_id_type=MESH,
        )

    def dv_rows(chunk, i):
        first = i * TOK
        total = None
        for h in range(GROUP_HEADS):
            cols = slice(h * PART + first, (h + 1) * PART)
            term = jnp.dot(
                expo[chunk, first : first + TOK, cols],
                cots[cols, :],
                preferred_element_type=jnp.float32,
            )
            total = term if total is None else total + term
        return total

    for slot, chunk in ((1, diagonal), (0, sibling)):
        for i in range(4):
            dv_out[slot, i * TOK : (i + 1) * TOK] = dv_rows(chunk, i).astype(jnp.bfloat16)
        dv_copy(slot).start()

    @pl.loop(0, 2)
    def _(step):
        chunk = jnp.where(step == 0, across, j)
        for i in range(4):
            dv_acc[step, i * TOK : (i + 1) * TOK] = dv_rows(chunk, i)

    dv_copy(1).wait_recv()
    dv_out[2] = (dv_acc[0] + dv_in[1].astype(jnp.float32)).astype(jnp.bfloat16)
    dv_copy(2).start()

    serve(0)

    x_wait(0)
    x_copy(4).start()
    x_wait(2)
    x_copy(5).start()

    serve(1)
    serve(2)

    local_copy(3).wait()

    def turn(half):
        for route in ((1, 4), (3, 5))[half]:
            x_wait(route)

        @pl.loop(0, X_HALF // 128)
        def _(i):
            first = pl.multiple_of(half * X_HALF + i * 128, 128)
            x_t[pl.ds(first, 128), :] = jnp.transpose(x_g[:, pl.ds(first, 128)])

    turn(0)

    dv_copy(0).wait_recv()
    dv_copy(2).wait_recv()
    dv_low = (
        dv_acc[1] + dv_in[0].astype(jnp.float32) + dv_in[2].astype(jnp.float32)
    ).astype(jnp.bfloat16)

    def gr_copy(slot, half):
        rows = pl.ds(half * 2 * ROWS, 2 * ROWS)
        return pltpu.make_async_remote_copy(
            src_ref=gr_out.at[slot, rows],
            dst_ref=gr_in.at[slot, rows],
            send_sem=gr_send.at[half, slot],
            recv_sem=gr_recv.at[half, slot],
            device_id=at(across if slot == 2 else sibling, g),
            device_id_type=MESH,
        )

    def rows_of(quarter, i):
        first = pl.multiple_of((i * QUARTERS + quarter) * ROWS, 16)
        return jnp.dot(x_t[pl.ds(first, ROWS), :], dv_low, preferred_element_type=jnp.float32)

    def spread(half):
        blocks = (2 * half, 2 * half + 1)
        rows = slice(half * 2 * ROWS, (half + 1) * 2 * ROWS)
        for slot, quarter in ((1, diagonal), (0, sibling)):
            for i in blocks:
                gr_out[slot, i * ROWS : (i + 1) * ROWS] = rows_of(quarter, i).astype(jnp.bfloat16)
            gr_copy(slot, half).start()
        for slot, quarter in ((0, across), (1, j)):
            for i in blocks:
                gr_acc[slot, i * ROWS : (i + 1) * ROWS] = rows_of(quarter, i)
        gr_copy(1, half).wait_recv()
        gr_out[2, rows] = (gr_acc[0, rows] + gr_in[1, rows].astype(jnp.float32)).astype(
            jnp.bfloat16
        )
        gr_copy(2, half).start()

    def own_copy(i):
        return pltpu.make_async_remote_copy(
            src_ref=sum_out.at[pl.ds(i * ROWS, ROWS)],
            dst_ref=grad.at[g],
            send_sem=own_send.at[i],
            recv_sem=own_recv.at[g],
            device_id=at(j, i),
            device_id_type=MESH,
        )

    def deliver(half):
        rows = slice(half * 2 * ROWS, (half + 1) * 2 * ROWS)
        total = gr_acc[1, rows]
        for slot in (0, 2):
            gr_copy(slot, half).wait_recv()
            total += gr_in[slot, rows].astype(jnp.float32)
        sum_out[rows] = total.astype(jnp.bfloat16)
        for i in (2 * half, 2 * half + 1):
            pl.when(g != i)(lambda: own_copy(i).start())

            @pl.when(g == i)
            def _(i=i):
                grad[i] = sum_out[i * ROWS : (i + 1) * ROWS]

    spread(0)
    turn(1)
    spread(1)
    deliver(0)
    deliver(1)

    for s in range(1, 4):
        peer = (g + s) % 4
        slot = grad.at[peer]
        pltpu.make_async_remote_copy(
            src_ref=slot,
            dst_ref=slot,
            send_sem=own_send.at[peer],
            recv_sem=own_recv.at[peer],
            device_id=at(j, peer),
            device_id_type=MESH,
        ).wait_recv()

    grad_copy = pltpu.make_async_copy(grad, grad_out, out_sem.at[0])
    grad_copy.start()

    for part in range(3):
        in_all(
            part,
            lambda n: bulk(part, n, deal_send.at[part], pick_recv.at[part]).wait_send(),
        )
        for role in range(2):
            has(part, cuts[role], lambda: swap_copy(part, role).wait_send())
    for part in range(3):
        in_all(
            part,
            lambda n: bulk(part, n, deal_send.at[part], pick_recv.at[part]).wait_recv(),
        )

    source_copy = pltpu.make_async_copy(source, source_out, out_sem.at[1])
    source_copy.start()

    for s in range(1, 4):
        for kind in range(3):
            group_copy(kind, s).wait_send()

        key_copy(s - 1).wait_send()
        dv_copy(s - 1).wait_send()
        gr_copy(s - 1, 0).wait_send()
        gr_copy(s - 1, 1).wait_send()
        own_copy((g + s) % 4).wait_send()
    for route in range(6):
        x_copy(route).wait_send()

    for part in range(3):
        for role in range(2):
            has(
                part,
                cuts[role],
                lambda: bulk(part, 15, pick_send.at[part], pick_recv.at[part]).wait_send(),
            )

    grad_copy.wait()
    source_copy.wait()


def plain_exchange(
    winners, w_in, m_in, v_in, source_out,
    w_own, m_own, v_own, state, dealt_0, dealt_1, dealt_2, picked_0, picked_1, picked_2, source,
    own_sem, out_sem, deal_send, deal_recv, pick_send, pick_recv,
):
    me = lax.axis_index("member")
    mine = lax.axis_index("fsdp")

    state_copies = [
        pltpu.make_async_copy(src, dst, own_sem.at[i])
        for i, (src, dst) in enumerate(((w_in, w_own), (m_in, m_own), (v_in, v_own)))
    ]
    for copy in state_copies:
        copy.start()

    barrier = pltpu.get_barrier_semaphore()

    @pl.loop(1, MEMBERS)
    def _(s):
        pl.semaphore_signal(
            barrier, inc=1, device_id={"member": (me + s) % MEMBERS}, device_id_type=MESH
        )

    for copy in state_copies:
        copy.wait()
    for band in range(8):
        cols = slice(band * 128, (band + 1) * 128)
        state[band, 0:ROWS] = w_own[:, cols]
        state[band, ROWS : 2 * ROWS] = m_own[:, cols].astype(jnp.bfloat16)
        state[band, 2 * ROWS : 3 * ROWS] = v_own[:, cols].astype(jnp.bfloat16)
    pl.semaphore_wait(barrier, MEMBERS - 1)

    core = mine % 2
    starts, sizes = (0, 48, 80), (48, 32, 16)
    dealt, picked = (dealt_0, dealt_1, dealt_2), (picked_0, picked_1, picked_2)

    def extra(member):
        return (member + 2 * core) % 4 == 1

    def sorts(member, part, action):
        if part < 2:
            action()
        else:
            pl.when(extra(member))(action)

    def place(ref, member, part):
        first = member % 4 * PIECE + starts[part] if part < 2 else 4 * PIECE
        return ref.at[member // 4, pl.ds(first, sizes[part])]

    def deal_copy(s, part):
        peer = (me + s) % MEMBERS
        return pltpu.make_async_remote_copy(
            src_ref=place(state, peer, part),
            dst_ref=dealt[part].at[me],
            send_sem=deal_send.at[part],
            recv_sem=deal_recv.at[part],
            device_id={"member": peer},
            device_id_type=MESH,
        )

    def all_of(part, count, send_sem, recv_sem):
        ref = dealt[part].at[pl.ds(0, count)]
        return pltpu.make_async_remote_copy(
            src_ref=ref,
            dst_ref=ref,
            send_sem=send_sem.at[part],
            recv_sem=recv_sem.at[part],
            device_id={"member": (me + 1) % MEMBERS},
            device_id_type=MESH,
        )

    def to_or_from_sorters(part, wait):
        if part < 2:
            wait(MEMBERS - 1)
        else:
            pl.when(extra(me))(lambda: wait(MEMBERS // 4 - 1))
            pl.when(jnp.logical_not(extra(me)))(lambda: wait(MEMBERS // 4))

    for part in range(3):

        @pl.loop(1, MEMBERS)
        def _(s):
            sorts((me + s) % MEMBERS, part, lambda: deal_copy(s, part).start())

    def keep(part):
        dealt[part][me] = place(state, me, part)[...]

    for part in range(3):
        sorts(me, part, lambda: keep(part))

    def pick_copy(s, part):
        peer = (me + s) % MEMBERS
        return pltpu.make_async_remote_copy(
            src_ref=picked[part].at[s],
            dst_ref=place(source, me, part),
            send_sem=pick_send.at[part],
            recv_sem=pick_recv.at[part],
            device_id={"member": peer},
            device_id_type=MESH,
        )

    def pick(part):
        def action():
            all_of(part, MEMBERS - 1, deal_send, deal_recv).wait_recv()

            @pl.loop(1, MEMBERS)
            def _(s):
                picked[part][s] = dealt[part][winners[(me + s) % MEMBERS]]
                pick_copy(s, part).start()

            place(source, me, part)[...] = dealt[part][winners[me]]

        sorts(me, part, action)

    for part in range(3):
        pick(part)
    for part in range(3):
        to_or_from_sorters(
            part, lambda count: all_of(part, count, deal_send, deal_recv).wait_send()
        )
    for part in range(3):
        to_or_from_sorters(
            part, lambda count: all_of(part, count, pick_send, pick_recv).wait_recv()
        )

    source_copy = pltpu.make_async_copy(source, source_out, out_sem.at[0])
    source_copy.start()
    for part in range(3):
        sorts(
            me, part, lambda: all_of(part, MEMBERS - 1, pick_send, pick_recv).wait_send()
        )
    source_copy.wait()


def adam_kernel(grad, source, new_w, new_m, new_v):
    for band in range(8):
        cols = slice(band * 128, (band + 1) * 128)
        lanes = slice(band % 2 * 128, band % 2 * 128 + 128)
        gradient = grad[band // 2, :, lanes].astype(jnp.float32)
        old_w = source[band, 0:ROWS].astype(jnp.float32)
        old_m = source[band, ROWS : 2 * ROWS].astype(jnp.float32)
        old_v = source[band, 2 * ROWS : 3 * ROWS].astype(jnp.float32)
        first = beta_one * old_m + (1.0 - beta_one) * gradient
        second = beta_two * old_v + (1.0 - beta_two) * gradient * gradient
        first_hat = first * (1.0 / (1.0 - beta_one**adam_step))
        second_hat = second * (1.0 / (1.0 - beta_two**adam_step))
        update = first_hat / (jnp.sqrt(second_hat) + adam_eps) + decay_rate * old_w
        new_w[:, cols] = (old_w - learning_rate * update).astype(jnp.bfloat16)
        new_m[:, cols] = first
        new_v[:, cols] = second


def local(inputs, queries, keys, cotangent, winners, weights, first_moment, second_moment):
    f32, bf16 = jnp.float32, jnp.bfloat16
    vmem = pl.BlockSpec(memory_space=pltpu.VMEM)
    hbm = pl.BlockSpec(memory_space=pltpu.HBM)
    dma = pltpu.SemaphoreType.DMA
    scratch = [
        pltpu.VMEM((QUARTERS, PART, HEAD_DIM), bf16),
        pltpu.VMEM((PART, GROUP_HEADS * HEAD_DIM), bf16),
        pltpu.VMEM((PART, GROUP_HEADS * HEAD_DIM), bf16),
        pltpu.VMEM((PART, FEAT), bf16),
        pltpu.VMEM((FEAT, PART), bf16),
        pltpu.VMEM((QUARTERS, PART, GROUP_HEADS * PART), bf16),
        pltpu.VMEM((1, GROUP_HEADS * PART), f32),
        pltpu.VMEM((GROUP_HEADS * PART, HEAD_DIM), bf16),
        pltpu.VMEM((2, PART, HEAD_DIM), f32),
        pltpu.VMEM((3, PART, HEAD_DIM), bf16),
        pltpu.VMEM((3, PART, HEAD_DIM), bf16),
        pltpu.VMEM((2, 4 * ROWS, HEAD_DIM), f32),
        pltpu.VMEM((3, 4 * ROWS, HEAD_DIM), bf16),
        pltpu.VMEM((3, 4 * ROWS, HEAD_DIM), bf16),
        pltpu.VMEM((4 * ROWS, HEAD_DIM), bf16),
        pltpu.VMEM((4, ROWS, HEAD_DIM), bf16),
    ]
    own_state = [
        pltpu.VMEM((ROWS, KVW), bf16),
        pltpu.VMEM((ROWS, KVW), f32),
        pltpu.VMEM((ROWS, KVW), f32),
        pltpu.VMEM((8, 3 * ROWS, 128), bf16),
    ]
    landing = pltpu.VMEM((8, 3 * ROWS, 128), bf16)
    parts = []
    for rows in (32, 48, 16):
        for count in (16, SLOTS, SLOTS, 16):
            parts += [pltpu.VMEM((count, rows, 128), bf16)] * 2
    parts += [pltpu.VMEM((30, rows, 128), bf16) for rows in (32, 48, 16)]
    state_args = (weights[0], first_moment[0], second_moment[0])
    state_shape = jax.ShapeDtypeStruct((8, 3 * ROWS, 128), bf16)
    smem = pl.BlockSpec(memory_space=pltpu.SMEM)
    grad, source, flag, same_winners = pl.pallas_call(
        kernel,
        out_shape=(
            jax.ShapeDtypeStruct((4, ROWS, HEAD_DIM), bf16),
            state_shape,
            jax.ShapeDtypeStruct((1,), jnp.int32),
            jax.ShapeDtypeStruct((MEMBERS,), jnp.int32),
        ),
        in_specs=[smem] + [hbm] * 7,
        out_specs=(hbm, hbm, smem, smem),
        scratch_shapes=scratch
        + own_state
        + [landing, pltpu.VMEM((8, 128), jnp.int32), pltpu.SMEM((8, 128), jnp.int32)]
        + [dma((4,)), dma((3,)), dma((3,)), dma((4, 4)), dma((4, 4))]
        + [dma((4,))] * 4
        + [dma((2, 4)), dma((2, 4)), dma((4,)), dma((4,)), dma((6,)), dma((6,))]
        + [dma((3,)), dma((3, 2)), dma((3, 2)), dma((3, 2)), dma((3,)), dma((3,))]
        + parts,
        compiler_params=pltpu.CompilerParams(
            collective_id=0, has_side_effects=True, vmem_limit_bytes=VMEM_LIMIT
        ),
        cost_estimate=pl.CostEstimate(
            flops=3_000_000_000, bytes_accessed=6_000_000, transcendentals=4_000_000
        ),
    )(winners, inputs[0], queries[0], keys[0], cotangent[0], *state_args)

    def step(grad, source):
        return pl.pallas_call(
            adam_kernel,
            out_shape=(
                jax.ShapeDtypeStruct((ROWS, KVW), bf16),
                jax.ShapeDtypeStruct((ROWS, KVW), f32),
                jax.ShapeDtypeStruct((ROWS, KVW), f32),
            ),
            in_specs=[vmem, vmem],
            out_specs=(vmem, vmem, vmem),
            compiler_params=pltpu.CompilerParams(vmem_limit_bytes=VMEM_LIMIT),
        )(grad, source)

    def crowded():
        all_source = pl.pallas_call(
            plain_exchange,
            out_shape=state_shape,
            in_specs=[smem] + [hbm] * 3,
            out_specs=hbm,
            scratch_shapes=own_state
            + [pltpu.VMEM((MEMBERS, rows, 128), bf16) for rows in (48, 32, 16)] * 2
            + [landing, dma((3,)), dma((1,))]
            + [dma((3,))] * 4,
            compiler_params=pltpu.CompilerParams(
                collective_id=1, has_side_effects=True, vmem_limit_bytes=VMEM_LIMIT
            ),
        )(same_winners, *state_args)
        return step(grad, all_source)

    outs = lax.cond(flag[0] > 0, crowded, lambda: step(grad, source))
    return tuple(out[None] for out in outs)


def solution(mesh):
    rows = P("member", "fsdp", None)
    return jax.shard_map(
        local,
        mesh=mesh,
        in_specs=(rows, rows, rows, rows, P(), rows, rows, rows),
        out_specs=(rows, rows, rows),
        check_vma=False,
    )
```
